32 devices in a mesh: groups: 2 (over x), lon: 16 (over z, y, core).
Axes of the slice: x: 2, y: 2, z: 4, core: 2. Of those that a mesh axis runs over, the one named last changes fastest.
Arguments:
- tokens: bfloat16 [64, 192, 1024], P(('groups', 'lon')), parts along dimension 0, may hold values from -32 to 32
- projection: bfloat16 [1024, 3072], replicated, may hold values from -1 to 1
- out_weight: bfloat16 [1024, 1024], replicated, may hold values from -1.5 to 1.5
- half_width: int32 [6], replicated, may hold values from 1 to 4, as said below
- neighbours: int32 [6, 2], replicated, may hold values from 0 to 5, as said below
Outputs:
- output: bfloat16 [64, 192, 1024], P(('groups', 'lon')), parts along dimension 0
The draws below stay inside these ranges and needn't reach their ends.
There are 2 independent parts, one for each index of `groups`. The reference program is written for one: setup_inputs(seed, part) draws one part's arguments, and reference() takes and returns one part's arrays. A program takes and returns all parts, laid end to end along the dimension named above; an argument that names none is the same for every part. Nothing has to cross between parts.
Inputs may be any that keep to these rules, and one draw needn't show every extreme that they name: `half_width`: exactly one latitude block has a half-width above 2, and its half-width is 4. `neighbours`: row b names 2 different latitude blocks, b among them.
All inputs are finite; a program needn't handle non-finite values.
Results may differ from the reference program's by a relative error of at most 0.0087.
Values may be sent and summed in bfloat16 or wider, within the bound.
No kernel may reach another device: no remote copies, remote signals or barrier semaphores. Data moves between devices by JAX's collectives and lax.ppermute only.
A program may use at most 128 MiB of HBM per device.

```python
import math
import jax
import jax.numpy as jnp
from jax import lax

D = 1024
HEADS = 16
LONB = 2
NLB = 6
NBR = 2
WMIN = 2
WMAX = 4
LAT = 192
LON = 32


def draw_tokens(key, part):
    key = jax.random.fold_in(key, 11)
    sub_keys = jax.random.split(key, 1)
    normals = jnp.clip(jax.random.normal(sub_keys[0], (LON, LAT, D), jnp.float32), -5.0, 5.0)
    return normals.astype(jnp.bfloat16)


def draw_projection(key, part):
    key = jax.random.fold_in(key, 12)
    sub_keys = jax.random.split(key, 3)
    root = D ** 0.5
    query_part = jnp.clip(jax.random.normal(sub_keys[0], (D, D), jnp.float32), -4.5, 4.5)
    key_part = jnp.clip(jax.random.normal(sub_keys[1], (D, D), jnp.float32), -4.5, 4.5)
    value_part = jnp.clip(jax.random.normal(sub_keys[2], (D, D), jnp.float32), -4.5, 4.5)
    return jnp.concatenate([query_part * (1.6 / root), key_part / root, value_part / root], axis=1).astype(jnp.bfloat16)


def draw_half_width(key, part):
    key = jax.random.fold_in(key, 13)
    sub_keys = jax.random.split(key, 2)
    widest = jax.random.randint(sub_keys[0], (), 0, NLB)
    others = jax.random.randint(sub_keys[1], (NLB,), 1, WMIN + 1)
    return jnp.where(jnp.arange(NLB) == widest, WMAX, others).astype(jnp.int32)


def draw_neighbours(key, part):
    key = jax.random.fold_in(key, 14)
    sub_keys = jax.random.split(key, 2)
    ranking = jax.random.randint(sub_keys[0], (NLB, NLB), 0, 1 << 20) * NLB + jnp.arange(NLB)[None, :]
    ranking = jnp.where(jnp.arange(NLB)[:, None] == jnp.arange(NLB)[None, :], -1, ranking)
    chosen = jnp.argsort(ranking, axis=1)[:, :NBR]
    rotation = jax.random.randint(sub_keys[1], (NLB, 1), 0, NBR)
    places = (jnp.arange(NBR)[None, :] + rotation) % NBR
    return jnp.take_along_axis(chosen, places, axis=1).astype(jnp.int32)


def centred(rng, extent, width, most, kind=jnp.bfloat16):
    entries = jax.random.normal(rng, extent, jnp.float32) * width
    return jnp.minimum(jnp.maximum(entries, -most), most).astype(kind)


def setup_inputs(seed: int = 0, part: int = 0) -> dict:
    splits = jax.random.split(jax.random.key(seed), 6)
    part_splits = jax.random.split(jax.random.fold_in(splits[5], part), 6)
    tokens = draw_tokens(jax.random.fold_in(jax.random.fold_in(splits[5], part), 71), part)
    projection = draw_projection(jax.random.fold_in(splits[5], 71), part)
    out_weight = centred(splits[2], (D, D), (D // 64) ** -0.5, 1.5)
    half_width = draw_half_width(jax.random.fold_in(splits[5], 71), part)
    neighbours = draw_neighbours(jax.random.fold_in(splits[5], 71), part)
    return {"tokens": tokens, "projection": projection, "out_weight": out_weight, "half_width": half_width, "neighbours": neighbours}


def reference(tokens, projection, out_weight, half_width, neighbours):
    lon_cells, lat_cells, model_width = tokens.shape
    lat_blocks = neighbours.shape[0]
    lat_size = lat_cells // lat_blocks
    lon_blocks = lon_cells // LONB
    block_rows = LONB * lat_size
    head_size = model_width // HEADS
    projected = jnp.dot(tokens.reshape(-1, model_width), projection, preferred_element_type=jnp.float32).astype(jnp.bfloat16)
    projected = projected.reshape(lon_blocks, LONB, lat_blocks, lat_size, 3 * model_width)
    projected = projected.transpose(0, 2, 1, 3, 4).reshape(lon_blocks, lat_blocks, block_rows, 3 * model_width)
    offsets = jnp.arange(-WMAX, WMAX + 1, dtype=jnp.int32)
    reaches = half_width[neighbours]
    visible = jnp.abs(offsets)[None, :, None] <= reaches[:, None, :]
    visible = jnp.repeat(visible.reshape(lat_blocks, -1), block_rows, axis=1)
    inverse_root = 1.0 / math.sqrt(head_size)

    def one_column(column):
        queries = projected[column, :, :, :model_width].astype(jnp.float32).reshape(lat_blocks, block_rows, HEADS, head_size)
        sources = ((column + offsets) % lon_blocks).astype(jnp.int32)
        key_band = projected[sources][:, :, :, model_width:]
        picked = key_band[:, neighbours]
        picked = picked.transpose(1, 0, 2, 3, 4).reshape(lat_blocks, -1, 2 * model_width).astype(jnp.float32)
        key_rows = picked[:, :, :model_width].reshape(lat_blocks, -1, HEADS, head_size)
        value_rows = picked[:, :, model_width:].reshape(lat_blocks, -1, HEADS, head_size)
        scores = jnp.einsum('bqhd,bkhd->bhqk', queries, key_rows) * inverse_root
        allowed = visible[:, None, None, :]
        row_max = lax.optimization_barrier(jnp.max(jnp.where(allowed, scores, -jnp.inf), axis=-1, keepdims=True))
        exponent = jnp.where(allowed, jnp.exp(scores - row_max), 0.0)
        row_total = lax.optimization_barrier(jnp.sum(exponent, axis=-1))
        weights = lax.optimization_barrier(exponent.astype(jnp.bfloat16)).astype(jnp.float32)
        attended = jnp.einsum('bhqk,bkhd->bqhd', weights, value_rows) / row_total.transpose(0, 2, 1)[..., None]
        return attended.astype(jnp.bfloat16).reshape(lat_blocks * block_rows, model_width)
    attended = lax.map(one_column, jnp.arange(lon_blocks, dtype=jnp.int32))
    output = jnp.dot(attended.reshape(-1, model_width), out_weight, preferred_element_type=jnp.float32).astype(jnp.bfloat16)
    output = output.reshape(lon_blocks, lat_blocks, LONB, lat_size, model_width).transpose(0, 2, 1, 3, 4)
    return output.reshape(lon_cells, lat_cells, model_width)
```

```python
import math

import jax
import jax.numpy as jnp
from jax import lax
from jax.experimental import pallas as pl
from jax.experimental.pallas import tpu as pltpu
from jax.sharding import PartitionSpec as P

HEADS = 16
HEAD = 64
PACK = 4
WIDE = PACK * HEAD
CHUNKS = 3
NEVER = -1e37
BF16 = jnp.bfloat16
F32 = jnp.float32
SCALE = math.log2(math.e) / math.sqrt(HEAD)
VMEM_LIMIT = 40 * 1024 * 1024


def lane_head(shape):
    return lax.broadcasted_iota(jnp.int32, shape, len(shape) - 1) // HEAD


def spread(packed):
    lane = lane_head((1, WIDE))
    return jnp.concatenate(
        [packed * (lane == h).astype(F32).astype(BF16) for h in range(PACK)], axis=0
    )


def gather_diagonal(full):
    lane = lane_head((HEAD, WIDE))
    total = full[:HEAD]
    for h in range(1, PACK):
        total = jnp.where(lane == h, full[h * HEAD : (h + 1) * HEAD], total)
    return total


def dot(a, b):
    return jnp.dot(a, b, preferred_element_type=F32)


def dot_nt(a, b):
    return lax.dot_general(a, b, (((1,), (1,)), ((), ())), preferred_element_type=F32)


def update(scores, values_t, carried):
    row_max, total, summed = carried
    new_max = jnp.maximum(row_max, jnp.max(scores, axis=0, keepdims=True))
    exponent = jnp.exp2((scores - new_max) * SCALE)
    factor = jnp.exp2((row_max - new_max) * SCALE)
    total = total * factor + jnp.sum(exponent, axis=0, keepdims=True)
    summed = summed * factor + gather_diagonal(dot(values_t, exponent.astype(BF16)))
    return new_max, total, summed


def halves(pair):
    lane = lax.broadcasted_iota(jnp.int32, pair.shape, 1)
    turned = pltpu.roll(pair, HEAD, 1)
    low = lane < HEAD
    zero = jnp.zeros_like(pair)
    first = (jnp.where(low, pair, zero), jnp.where(low, zero, turned))
    second = (jnp.where(low, turned, zero), jnp.where(low, zero, pair))
    return first, second


def first_kernel(nbr, x, s, w, qc, m_out, l_out, acc, wvt, own, both, keys, vals):
    nlb = nbr.shape[0]
    span = x.shape[1] // nlb
    lon = x.shape[0]
    rows = lon * span
    width = x.shape[2]
    groups = width // WIDE
    for c in range(nlb):
        for o in range(lon):
            part = x[o, c * span : (c + 1) * span, :]
            own[c * rows + o * span : c * rows + (o + 1) * span, :] = part
            at = 2 * c * rows + o * span
            both[at : at + span, :] = part
            both[at + rows : at + rows + span, :] = s[o, c * span : (c + 1) * span, :]

    def turn(i, _):
        at = pl.multiple_of(i * 256, 256)
        wvt[pl.ds(at, 256), :] = w[:, pl.ds(2 * width + at, 256)].T
        return 0

    lax.fori_loop(0, width // 256, turn, 0)

    def project(g, _):
        at = pl.multiple_of(g * WIDE, WIDE)
        q = dot(own[...], w[:, pl.ds(at, WIDE)]).astype(BF16).astype(F32)
        for b in range(nlb):
            qt = q[b * rows : (b + 1) * rows, :].T
            qc[b * groups + g] = jnp.concatenate(
                [qt[h * HEAD : (h + 1) * HEAD, :] for h in range(PACK)], axis=1
            ).astype(BF16)
        k = dot(both[...], w[:, pl.ds(width + at, WIDE)]).astype(BF16)
        v = dot_nt(wvt[pl.ds(at, WIDE), :], both[...]).astype(BF16)
        for c in range(nlb):
            keys[c, g] = k[2 * c * rows : 2 * (c + 1) * rows, :]
            vals[c, g] = v[:, 2 * c * rows : 2 * (c + 1) * rows]
        return 0

    lax.fori_loop(0, groups, project, 0)

    def attend(b, _):
        c0, c1 = nbr[b, 0], nbr[b, 1]
        for g in range(groups):
            t = b * groups + g
            k = jnp.concatenate([keys[c0, g], keys[c1, g]], axis=0)
            v = jnp.concatenate([vals[c0, g], vals[c1, g]], axis=1)
            scores = dot(k, spread(qc[t]))
            row_max = jnp.max(scores, axis=0, keepdims=True)
            exponent = jnp.exp2((scores - row_max) * SCALE)
            m_out[t] = row_max
            l_out[t] = jnp.sum(exponent, axis=0, keepdims=True)
            acc[t] = gather_diagonal(dot(v, exponent.astype(BF16)))
        return 0

    lax.fori_loop(0, nlb, attend, 0)


def fill_tokens(chunks, tokens, rows, span, lon):
    at = 0
    for chunk in chunks:
        for c in range(chunk.shape[1] // span):
            for o in range(lon):
                tokens[at : at + span, :] = chunk[o, c * span : (c + 1) * span, :]
                at += span


def wide_update(nbr, wide, qc, wkeys, wvals, carried_refs, groups):
    m, l, acc = carried_refs

    def attend(b, _):
        @pl.when((nbr[b, 0] == wide[0]) | (nbr[b, 1] == wide[0]))
        def _():
            for g in range(groups):
                t = b * groups + g
                scores = dot(wkeys[g], spread(qc[t]))
                m[t], l[t], acc[t] = update(scores, wvals[g], (m[t], l[t], acc[t]))

        return 0

    lax.fori_loop(0, nbr.shape[0], attend, 0)


def second_kernel(nbr, wide, f0, f1, f2, wf, wb, w, wvt, qc, m_in, l_in, acc_in,
                  fkeys, fvals, m, l, acc, tokens, wkeys, wvals):
    nlb = nbr.shape[0]
    lon, rows_c, width = f0.shape
    span = rows_c * CHUNKS // nlb
    rows = lon * span
    groups = width // WIDE
    fill_tokens((f0, f1, f2), tokens, rows, span, lon)
    tokens[nlb * rows : (nlb + 1) * rows, :] = wf[...]
    tokens[(nlb + 1) * rows :, :] = wb[...]
    m[...] = m_in[...]
    l[...] = l_in[...]
    acc[...] = acc_in[...]

    def project(g, _):
        at = pl.multiple_of(g * WIDE, WIDE)
        k = dot(tokens[...], w[:, pl.ds(at, WIDE)]).astype(BF16)
        v = dot_nt(wvt[pl.ds(at, WIDE), :], tokens[...])
        for c in range(0, nlb, 2):
            first, second = halves(v[:, c * rows : (c + 2) * rows])
            fkeys[c, g] = k[c * rows : (c + 1) * rows, :]
            fkeys[c + 1, g] = k[(c + 1) * rows : (c + 2) * rows, :]
            fvals[c, g] = first[0].astype(BF16)
            fvals[c + 1, g] = second[0].astype(BF16)
        wkeys[g] = k[nlb * rows :, :]
        wvals[g] = v[:, nlb * rows :].astype(BF16)
        return 0

    lax.fori_loop(0, groups, project, 0)
    wide_update(nbr, wide, qc, wkeys, wvals, (m, l, acc), groups)


def third_kernel(nbr, hw, g0, g1, g2, w, wvt, qc, fkeys, fvals, m_in, l_in, acc_in,
                 m, l, acc, tokens, keys, vals):
    nlb = nbr.shape[0]
    lon, rows_c, width = g0.shape
    span = rows_c * CHUNKS // nlb
    rows = lon * span
    groups = width // WIDE
    fill_tokens((g0, g1, g2), tokens, rows, span, lon)

    def project(g, _):
        at = pl.multiple_of(g * WIDE, WIDE)
        k = dot(tokens[...], w[:, pl.ds(at, WIDE)]).astype(BF16)
        v = dot_nt(wvt[pl.ds(at, WIDE), :], tokens[...])
        for c in range(0, nlb, 2):
            first, second = halves(v[:, c * rows : (c + 2) * rows])
            for i, part in ((c, first), (c + 1, second)):
                keys[i, g, :rows] = fkeys[i, g]
                keys[i, g, rows:] = k[i * rows : (i + 1) * rows, :]
                vals[i, g] = fvals[i, g] + part[1].astype(BF16)
        return 0

    lax.fori_loop(0, groups, project, 0)

    def attend(b, _):
        c0, c1 = nbr[b, 0], nbr[b, 1]
        seen0, seen1 = hw[c0] >= 2, hw[c1] >= 2
        for g in range(groups):
            t = b * groups + g
            q = spread(qc[t])
            k = jnp.concatenate([keys[c0, g], keys[c1, g]], axis=0)
            v = jnp.concatenate([vals[c0, g], vals[c1, g]], axis=1)
            scores = dot(k, q)
            scores = jnp.concatenate(
                [
                    jnp.where(seen0, scores[: 2 * rows], NEVER),
                    jnp.where(seen1, scores[2 * rows :], NEVER),
                ],
                axis=0,
            )
            m[t], l[t], acc[t] = update(scores, v, (m_in[t], l_in[t], acc_in[t]))
        return 0

    lax.fori_loop(0, nlb, attend, 0)


def payload_kernel(flags, f0, f1, f2, g0, g1, g2, wf, wb, out):
    lon, rows_c, width = f0.shape
    span = wf.shape[0] // lon
    per = rows_c // span
    fs, gs = (f0, f1, f2), (g0, g1, g2)
    base = CHUNKS * lon * rows_c
    rows = lon * span

    def fill(sent, other, wide_sent):
        for j in range(CHUNKS):
            for c in range(per):
                for o in range(lon):
                    at = ((j * per + c) * lon + o) * span
                    out[at : at + span, :] = sent[j][o, c * span : (c + 1) * span, :]
        out[base : base + rows, :] = wide_sent[...]
        for j in range(CHUNKS):
            for c in range(per):

                @pl.when(flags[1] == j * per + c)
                def _(j=j, c=c):
                    for o in range(lon):
                        at = base + rows + o * span
                        out[at : at + span, :] = other[j][o, c * span : (c + 1) * span, :]

    @pl.when(flags[0] == 0)
    def _():
        fill(fs, gs, wb)

    @pl.when(flags[0] != 0)
    def _():
        fill(gs, fs, wf)


def fourth_kernel(nbr, wide, e, w, wvt, wout, qc, m_in, l_in, acc_in, out,
                  m, l, acc, keys, vals, wkeys, wvals, attended):
    nlb = nbr.shape[0]
    width = e.shape[1]
    rows = e.shape[0] // (nlb + 2)
    lon = out.shape[0]
    span = rows // lon
    groups = width // WIDE

    def project(g, _):
        at = pl.multiple_of(g * WIDE, WIDE)
        k = dot(e[...], w[:, pl.ds(at, WIDE)]).astype(BF16)
        v = dot_nt(wvt[pl.ds(at, WIDE), :], e[...])
        for c in range(0, nlb, 2):
            first, second = halves(v[:, c * rows : (c + 2) * rows])
            for i, part in ((c, first), (c + 1, second)):
                keys[i, g] = k[i * rows : (i + 1) * rows, :]
                vals[0, i, g] = part[0].astype(BF16)
                vals[1, i, g] = part[1].astype(BF16)
        wkeys[g] = k[nlb * rows :, :]
        wvals[g] = v[:, nlb * rows :].astype(BF16)
        return 0

    lax.fori_loop(0, groups, project, 0)

    def attend(b, _):
        c0, c1 = nbr[b, 0], nbr[b, 1]
        for g in range(groups):
            t = b * groups + g
            k = jnp.concatenate([keys[c0, g], keys[c1, g]], axis=0)
            v = vals[0, c0, g] + vals[1, c1, g]
            scores = dot(k, spread(qc[t]))
            m[t], l[t], acc[t] = update(scores, v, (m_in[t], l_in[t], acc_in[t]))
        return 0

    lax.fori_loop(0, nlb, attend, 0)
    wide_update(nbr, wide, qc, wkeys, wvals, (m, l, acc), groups)

    def finish(b, _):
        for g in range(groups):
            t = b * groups + g
            done = (acc[t] / l[t]).T
            attended[pl.ds(pl.multiple_of(b * rows, rows), rows), g * WIDE : (g + 1) * WIDE] = (
                jnp.concatenate(
                    [done[h * HEAD : (h + 1) * HEAD, :] for h in range(PACK)], axis=1
                ).astype(BF16)
            )
        return 0

    lax.fori_loop(0, nlb, finish, 0)

    def product(g, _):
        at = pl.multiple_of(g * WIDE, WIDE)
        r = dot(attended[...], wout[:, pl.ds(at, WIDE)]).astype(BF16)
        for b in range(nlb):
            for o in range(lon):
                out[o, b * span : (b + 1) * span, pl.ds(at, WIDE)] = r[
                    b * rows + o * span : b * rows + (o + 1) * span, :
                ]
        return 0

    lax.fori_loop(0, groups, product, 0)


def call(kernel, scalars, arrays, outs, scratch, flops):
    smem = pl.BlockSpec(memory_space=pltpu.SMEM)
    vmem = pl.BlockSpec(memory_space=pltpu.VMEM)
    single = not isinstance(outs, (list, tuple))
    moved = sum(a.size * a.dtype.itemsize for a in arrays)
    return pl.pallas_call(
        kernel,
        out_shape=outs,
        in_specs=[smem] * len(scalars) + [vmem] * len(arrays),
        out_specs=vmem if single else [vmem] * len(outs),
        scratch_shapes=scratch,
        compiler_params=pltpu.CompilerParams(vmem_limit_bytes=VMEM_LIMIT),
        cost_estimate=pl.CostEstimate(flops=flops, bytes_accessed=moved, transcendentals=0),
    )(*scalars, *arrays)


def per_device(tokens, projection, out_weight, half_width, neighbours):
    lon, lat, width = tokens.shape
    nlb = neighbours.shape[0]
    span = lat // nlb
    rows = lon * span
    groups = width // WIDE
    tiles = nlb * groups
    count = lax.axis_size("lon")
    here = lax.axis_index("lon")
    devices = range(count)

    def permute(block, step):
        return lax.ppermute(block, "lon", [(i, step(i) % count) for i in devices])

    def sibling(i):
        return i ^ 1

    def across(i):
        return i ^ 2

    def onward(i):
        return i - 4 if i & 2 else i + 4

    def backward(i):
        return i + 4 if i & 2 else i - 4

    widest = jnp.argmax(half_width).astype(jnp.int32)
    wide = widest.reshape(1)
    beside = permute(tokens, sibling)
    part = lat // CHUNKS
    f = [permute(tokens[:, j * part : (j + 1) * part, :], across) for j in range(CHUNKS)]
    band = lax.dynamic_slice(tokens, (0, widest * span, 0), (lon, span, width)).reshape(rows, width)
    wf = permute(band, onward)
    wb = permute(band, backward)
    g = [permute(block, onward) for block in f]

    tile = (tiles, HEAD, WIDE)
    row = (tiles, 1, WIDE)
    carried_shapes = [
        jax.ShapeDtypeStruct(row, F32),
        jax.ShapeDtypeStruct(row, F32),
        jax.ShapeDtypeStruct(tile, F32),
    ]
    qc, m, l, acc, wvt = call(
        first_kernel,
        (neighbours,),
        (tokens, beside, projection),
        [jax.ShapeDtypeStruct(tile, BF16)] + carried_shapes + [jax.ShapeDtypeStruct((width, width), BF16)],
        [
            pltpu.VMEM((nlb * rows, width), BF16),
            pltpu.VMEM((2 * nlb * rows, width), BF16),
            pltpu.VMEM((nlb, groups, 2 * rows, WIDE), BF16),
            pltpu.VMEM((nlb, groups, WIDE, 2 * rows), BF16),
        ],
        6_000_000_000,
    )
    wk = projection[:, width : 2 * width]
    fkeys, fvals, m, l, acc = call(
        second_kernel,
        (neighbours, wide),
        (*f, wf, wb, wk, wvt, qc, m, l, acc),
        [
            jax.ShapeDtypeStruct((nlb, groups, rows, WIDE), BF16),
            jax.ShapeDtypeStruct((nlb, groups, WIDE, 2 * rows), BF16),
        ]
        + carried_shapes,
        [
            pltpu.VMEM(((nlb + 2) * rows, width), BF16),
            pltpu.VMEM((groups, 2 * rows, WIDE), BF16),
            pltpu.VMEM((groups, WIDE, 2 * rows), BF16),
        ],
        3_000_000_000,
    )
    kind = (here ^ (here >> 1)) & 1
    flags = jnp.stack([kind.astype(jnp.int32), widest])
    e = call(
        payload_kernel,
        (flags,),
        (*f, *g, wf, wb),
        jax.ShapeDtypeStruct(((nlb + 2) * rows, width), BF16),
        [],
        1_000_000,
    )
    e = permute(e, sibling)
    m, l, acc = call(
        third_kernel,
        (neighbours, half_width),
        (*g, wk, wvt, qc, fkeys, fvals, m, l, acc),
        carried_shapes,
        [
            pltpu.VMEM((nlb * rows, width), BF16),
            pltpu.VMEM((nlb, groups, 2 * rows, WIDE), BF16),
            pltpu.VMEM((nlb, groups, WIDE, 2 * rows), BF16),
        ],
        4_000_000_000,
    )
    return call(
        fourth_kernel,
        (neighbours, wide),
        (e, wk, wvt, out_weight, qc, m, l, acc),
        jax.ShapeDtypeStruct(tokens.shape, BF16),
        [
            pltpu.VMEM(row, F32),
            pltpu.VMEM(row, F32),
            pltpu.VMEM(tile, F32),
            pltpu.VMEM((nlb, groups, rows, WIDE), BF16),
            pltpu.VMEM((2, nlb, groups, WIDE, 2 * rows), BF16),
            pltpu.VMEM((groups, 2 * rows, WIDE), BF16),
            pltpu.VMEM((groups, WIDE, 2 * rows), BF16),
            pltpu.VMEM((nlb * rows, width), BF16),
        ],
        4_000_000_000,
    )


def solution(mesh):
    return jax.shard_map(
        per_device,
        mesh=mesh,
        in_specs=(P(("groups", "lon"), None, None), P(), P(), P(), P()),
        out_specs=P(("groups", "lon"), None, None),
        check_vma=False,
    )
```

```python
import math

import jax
import jax.numpy as jnp
from jax import lax
from jax.experimental import pallas as pl
from jax.experimental.pallas import tpu as pltpu
from jax.sharding import PartitionSpec as P

HEADS = 16
HEAD = 64
PACK = 4
WIDE = PACK * HEAD
CHUNKS = 3
NEVER = -1e37
BF16 = jnp.bfloat16
F32 = jnp.float32
SCALE = math.log2(math.e) / math.sqrt(HEAD)
VMEM_LIMIT = 40 * 1024 * 1024


def lane_head(shape):
    return lax.broadcasted_iota(jnp.int32, shape, len(shape) - 1) // HEAD


def spread(packed):
    lane = lane_head((1, WIDE))
    return jnp.concatenate(
        [packed * (lane == h).astype(F32).astype(BF16) for h in range(PACK)], axis=0
    )


def gather_diagonal(full):
    lane = lane_head((HEAD, WIDE))
    total = full[:HEAD]
    for h in range(1, PACK):
        total = jnp.where(lane == h, full[h * HEAD : (h + 1) * HEAD], total)
    return total


def dot(a, b):
    return jnp.dot(a, b, preferred_element_type=F32)


def dot_nt(a, b):
    return lax.dot_general(a, b, (((1,), (1,)), ((), ())), preferred_element_type=F32)


def update(scores, values_t, carried):
    row_max, total, summed = carried
    new_max = jnp.maximum(row_max, jnp.max(scores, axis=0, keepdims=True))
    exponent = jnp.exp2((scores - new_max) * SCALE)
    factor = jnp.exp2((row_max - new_max) * SCALE)
    total = total * factor + jnp.sum(exponent, axis=0, keepdims=True)
    summed = summed * factor + gather_diagonal(dot(values_t, exponent.astype(BF16)))
    return new_max, total, summed


def halves(pair):
    lane = lax.broadcasted_iota(jnp.int32, pair.shape, 1)
    turned = pltpu.roll(pair, HEAD, 1)
    low = lane < HEAD
    zero = jnp.zeros_like(pair)
    first = (jnp.where(low, pair, zero), jnp.where(low, zero, turned))
    second = (jnp.where(low, turned, zero), jnp.where(low, zero, pair))
    return first, second


def widest_of(hw):
    best, where = hw[0], 0
    for c in range(1, hw.shape[0]):
        larger = hw[c] > best
        best = jnp.where(larger, hw[c], best)
        where = jnp.where(larger, c, where)
    return where


def project_values(wvt, tokens, g, blocks, rows):
    v = dot_nt(wvt[g * WIDE : (g + 1) * WIDE, :], tokens)
    parts = []
    for c in range(0, blocks, 2):
        for left, right in halves(v[:, c * rows : (c + 2) * rows]):
            parts.append((left.astype(BF16), right.astype(BF16)))
    return parts, v[:, blocks * rows :].astype(BF16)


def columns(which, g, width):
    return slice(which * width + g * WIDE, which * width + (g + 1) * WIDE)


def prepare_kernel(hw, x, f0, f1, f2, band):
    lon, lat, width = x.shape
    span = lat // hw.shape[0]
    out = (f0, f1, f2)
    per = hw.shape[0] // CHUNKS
    for c in range(hw.shape[0]):
        for o in range(lon):
            at = ((c % per) * lon + o) * span
            out[c // per][at : at + span, :] = x[o, c * span : (c + 1) * span, :]
    begin = pl.multiple_of(widest_of(hw) * span, span)
    for o in range(lon):
        band[o * span : (o + 1) * span, :] = x[o, pl.ds(begin, span), :]


def own_kernel(x, w, qc, keys, vals, wvt, own):
    lon, _, width = x.shape
    nlb, groups, rows, _ = keys.shape
    span = rows // lon
    for c in range(nlb):
        for o in range(lon):
            own[c * rows + o * span : c * rows + (o + 1) * span, :] = x[o, c * span : (c + 1) * span, :]
    for i in range(0, width, WIDE):
        wvt[i : i + WIDE, :] = w[:, 2 * width + i : 2 * width + i + WIDE].T
    for g in range(groups):
        q = dot(own[...], w[:, columns(0, g, width)]).astype(BF16).astype(F32)
        for b in range(nlb):
            qt = q[b * rows : (b + 1) * rows, :].T
            qc[b * groups + g] = jnp.concatenate(
                [qt[h * HEAD : (h + 1) * HEAD, :] for h in range(PACK)], axis=1
            ).astype(BF16)
        k = dot(own[...], w[:, columns(1, g, width)]).astype(BF16)
        parts, _ = project_values(wvt, own[...], g, nlb, rows)
        for c in range(nlb):
            keys[c, g] = k[c * rows : (c + 1) * rows, :]
            vals[c, g] = parts[c][0]


def near_kernel(nbr, s, w, wvt, qc, okeys, ovals, m, l, acc, near, keys, vals):
    lon, _, width = s.shape
    nlb, groups, rows, _ = okeys.shape
    span = rows // lon
    for c in range(nlb):
        for o in range(lon):
            near[c * rows + o * span : c * rows + (o + 1) * span, :] = s[o, c * span : (c + 1) * span, :]
    for g in range(groups):
        k = dot(near[...], w[:, columns(1, g, width)]).astype(BF16)
        parts, _ = project_values(wvt, near[...], g, nlb, rows)
        for c in range(nlb):
            keys[c, g, :rows] = okeys[c, g]
            keys[c, g, rows:] = k[c * rows : (c + 1) * rows, :]
            vals[c, g] = ovals[c, g] + parts[c][1]
    for b in range(nlb):
        c0, c1 = nbr[b, 0], nbr[b, 1]
        for g in range(groups):
            t = b * groups + g
            k = jnp.concatenate([keys[c0, g], keys[c1, g]], axis=0)
            v = jnp.concatenate([vals[c0, g], vals[c1, g]], axis=1)
            scores = dot(k, spread(qc[t]))
            row_max = jnp.max(scores, axis=0, keepdims=True)
            exponent = jnp.exp2((scores - row_max) * SCALE)
            m[t] = row_max
            l[t] = jnp.sum(exponent, axis=0, keepdims=True)
            acc[t] = gather_diagonal(dot(v, exponent.astype(BF16)))


def project_far(tokens, w, wvt, keys, vals, wkeys, wvals):
    nlb, groups, rows, _ = keys.shape
    width = tokens.shape[1]
    for g in range(groups):
        k = dot(tokens[...], w[:, columns(1, g, width)]).astype(BF16)
        parts, rest = project_values(wvt, tokens[...], g, nlb, rows)
        for c in range(nlb):
            keys[c, g] = k[c * rows : (c + 1) * rows, :]
            vals[0, c, g] = parts[c][0]
            vals[1, c, g] = parts[c][1]
        if wkeys is not None:
            wkeys[g] = k[nlb * rows :, :]
            wvals[g] = rest


def attend_far(nbr, seen, wide, qc, keys, vals, wkeys, wvals, before, after):
    nlb, groups, rows, _ = keys.shape
    for b in range(nlb):
        c0, c1 = nbr[b, 0], nbr[b, 1]
        for g in range(groups):
            t = b * groups + g
            q = spread(qc[t])
            ks = [keys[c0, g], keys[c1, g]]
            v = vals[0, c0, g] + vals[1, c1, g]
            if wkeys is not None:
                ks.append(wkeys[g])
                v = jnp.concatenate([v, wvals[g]], axis=1)
            scores = dot(jnp.concatenate(ks, axis=0), q)
            pieces = [scores[:rows], scores[rows : 2 * rows], scores[2 * rows :]]
            if seen is not None:
                pieces[0] = jnp.where(seen[c0] >= 2, pieces[0], NEVER)
                pieces[1] = jnp.where(seen[c1] >= 2, pieces[1], NEVER)
            if wkeys is None:
                pieces = pieces[:2]
            else:
                pieces[2] = jnp.where((c0 == wide) | (c1 == wide), pieces[2], NEVER)
            scores = jnp.concatenate(pieces, axis=0)
            m, l, acc = update(scores, v, tuple(r[t] for r in before))
            after[0][t], after[1][t], after[2][t] = m, l, acc


def across_kernel(nbr, hw, f0, f1, f2, wf, wb, w, wvt, qc, m_in, l_in, acc_in,
                  m, l, acc, tokens, keys, vals, wkeys, wvals):
    at = 0
    for part in (f0, f1, f2, wf, wb):
        tokens[at : at + part.shape[0], :] = part[...]
        at += part.shape[0]
    project_far(tokens, w, wvt, keys, vals, wkeys, wvals)
    attend_far(nbr, hw, widest_of(hw), qc, keys, vals, wkeys, wvals, (m_in, l_in, acc_in), (m, l, acc))


def onward_kernel(nbr, hw, g0, g1, g2, w, wvt, qc, m_in, l_in, acc_in, m, l, acc, tokens, keys, vals):
    at = 0
    for part in (g0, g1, g2):
        tokens[at : at + part.shape[0], :] = part[...]
        at += part.shape[0]
    project_far(tokens, w, wvt, keys, vals, None, None)
    attend_far(nbr, hw, None, qc, keys, vals, None, None, (m_in, l_in, acc_in), (m, l, acc))


def payload_kernel(hw, f0, f1, f2, g0, g1, g2, wf, wb, _, out):
    here = lax.axis_index("lon")
    wide = widest_of(hw)
    size = f0.shape[0]
    rows = wf.shape[0]
    per = size // rows
    base = CHUNKS * size

    def fill(sent, other, wide_sent):
        for j in range(CHUNKS):
            out[j * size : (j + 1) * size, :] = sent[j][...]
        out[base : base + rows, :] = wide_sent[...]
        for c in range(CHUNKS * per):

            @pl.when(wide == c)
            def _(c=c):
                at = (c % per) * rows
                out[base + rows :, :] = other[c // per][at : at + rows, :]

    kind = (here ^ (here >> 1)) & 1

    @pl.when(kind == 0)
    def _():
        fill((f0, f1, f2), (g0, g1, g2), wb)

    @pl.when(kind != 0)
    def _():
        fill((g0, g1, g2), (f0, f1, f2), wf)


def last_kernel(nbr, hw, e, w, wvt, wout, qc, m_in, l_in, acc_in, out,
                m, l, acc, keys, vals, wkeys, wvals, attended):
    nlb, groups, rows, _ = keys.shape
    lon = out.shape[0]
    span = rows // lon
    project_far(e, w, wvt, keys, vals, wkeys, wvals)
    attend_far(nbr, None, widest_of(hw), qc, keys, vals, wkeys, wvals, (m_in, l_in, acc_in), (m, l, acc))
    for b in range(nlb):
        for g in range(groups):
            t = b * groups + g
            done = (acc[t] / l[t]).T
            attended[b * rows : (b + 1) * rows, g * WIDE : (g + 1) * WIDE] = jnp.concatenate(
                [done[h * HEAD : (h + 1) * HEAD, :] for h in range(PACK)], axis=1
            ).astype(BF16)
    for g in range(groups):
        r = dot(attended[...], wout[:, columns(0, g, 0)]).astype(BF16)
        for b in range(nlb):
            for o in range(lon):
                at = b * rows + o * span
                out[o, b * span : (b + 1) * span, g * WIDE : (g + 1) * WIDE] = r[at : at + span, :]


def call(kernel, scalars, arrays, outs, scratch, flops, unread=0):
    smem = pl.BlockSpec(memory_space=pltpu.SMEM)
    vmem = pl.BlockSpec(memory_space=pltpu.VMEM)
    single = not isinstance(outs, (list, tuple))
    moved = sum(a.size * a.dtype.itemsize for a in arrays)
    specs = [vmem] * (len(arrays) - unread) + [pl.BlockSpec(memory_space=pl.ANY)] * unread
    return pl.pallas_call(
        kernel,
        out_shape=outs,
        in_specs=[smem] * len(scalars) + specs,
        out_specs=vmem if single else [vmem] * len(outs),
        scratch_shapes=scratch,
        compiler_params=pltpu.CompilerParams(vmem_limit_bytes=VMEM_LIMIT),
        cost_estimate=pl.CostEstimate(flops=flops, bytes_accessed=moved, transcendentals=0),
    )(*scalars, *arrays)


def after(value, *others):
    return lax.optimization_barrier((value, *others))[0]


def per_device(tokens, projection, out_weight, half_width, neighbours):
    lon, lat, width = tokens.shape
    nlb = neighbours.shape[0]
    span = lat // nlb
    rows = lon * span
    groups = width // WIDE
    tiles = nlb * groups
    count = lax.axis_size("lon")
    devices = range(count)

    def permute(block, step):
        return lax.ppermute(block, "lon", [(i, step(i) % count) for i in devices])

    def sibling(i):
        return i ^ 1

    def across(i):
        return i ^ 2

    def onward(i):
        return i - 4 if i & 2 else i + 4

    def backward(i):
        return i + 4 if i & 2 else i - 4

    tile = (tiles, HEAD, WIDE)
    row = (tiles, 1, WIDE)
    carried_shapes = [
        jax.ShapeDtypeStruct(row, F32),
        jax.ShapeDtypeStruct(row, F32),
        jax.ShapeDtypeStruct(tile, F32),
    ]
    key_scratch = pltpu.VMEM((nlb, groups, rows, WIDE), BF16)
    val_scratch = pltpu.VMEM((2, nlb, groups, WIDE, 2 * rows), BF16)
    wide_scratch = [
        pltpu.VMEM((groups, 2 * rows, WIDE), BF16),
        pltpu.VMEM((groups, WIDE, 2 * rows), BF16),
    ]

    beside = permute(tokens, sibling)
    chunk = jax.ShapeDtypeStruct((nlb * rows // CHUNKS, width), BF16)
    *parts, band = call(
        prepare_kernel,
        (half_width,),
        (tokens,),
        [chunk] * CHUNKS + [jax.ShapeDtypeStruct((rows, width), BF16)],
        [],
        1_000_000,
    )
    f = [permute(part, across) for part in parts]
    wf = permute(band, onward)
    wb = permute(band, backward)
    g0 = permute(f[0], onward)
    qc, okeys, ovals, wvt = call(
        own_kernel,
        (),
        (after(tokens, f[0]), projection),
        [
            jax.ShapeDtypeStruct(tile, BF16),
            jax.ShapeDtypeStruct((nlb, groups, rows, WIDE), BF16),
            jax.ShapeDtypeStruct((nlb, groups, WIDE, 2 * rows), BF16),
            jax.ShapeDtypeStruct((width, width), BF16),
        ],
        [pltpu.VMEM((nlb * rows, width), BF16)],
        4_000_000_000,
    )
    g1 = permute(after(f[1], qc), onward)
    m, l, acc = call(
        near_kernel,
        (neighbours,),
        (after(beside, f[1]), projection, wvt, qc, okeys, ovals),
        carried_shapes,
        [
            pltpu.VMEM((nlb * rows, width), BF16),
            pltpu.VMEM((nlb, groups, 2 * rows, WIDE), BF16),
            pltpu.VMEM((nlb, groups, WIDE, 2 * rows), BF16),
        ],
        4_000_000_000,
    )
    g2 = permute(after(f[2], m), onward)
    m, l, acc = call(
        across_kernel,
        (neighbours, half_width),
        (*f, wf, wb, projection, wvt, qc, m, l, acc),
        carried_shapes,
        [pltpu.VMEM(((nlb + 2) * rows, width), BF16), key_scratch, val_scratch, *wide_scratch],
        6_000_000_000,
    )
    e = call(
        payload_kernel,
        (half_width,),
        (*f, g0, g1, g2, wf, wb, m),
        jax.ShapeDtypeStruct(((nlb + 2) * rows, width), BF16),
        [],
        1_000_000,
        unread=1,
    )
    e = permute(e, sibling)
    m, l, acc = call(
        onward_kernel,
        (neighbours, half_width),
        (g0, g1, g2, projection, wvt, qc, m, l, acc),
        carried_shapes,
        [pltpu.VMEM((nlb * rows, width), BF16), key_scratch, val_scratch],
        4_000_000_000,
    )
    return call(
        last_kernel,
        (neighbours, half_width),
        (e, projection, wvt, out_weight, qc, m, l, acc),
        jax.ShapeDtypeStruct(tokens.shape, BF16),
        [
            pltpu.VMEM(row, F32),
            pltpu.VMEM(row, F32),
            pltpu.VMEM(tile, F32),
            key_scratch,
            val_scratch,
            *wide_scratch,
            pltpu.VMEM((nlb * rows, width), BF16),
        ],
        6_000_000_000,
    )


def solution(mesh):
    return jax.shard_map(
        per_device,
        mesh=mesh,
        in_specs=(P(("groups", "lon"), None, None), P(), P(), P(), P()),
        out_specs=P(("groups", "lon"), None, None),
        check_vma=False,
    )
```

```python
import math

import jax
import jax.numpy as jnp
from jax import lax
from jax.experimental import pallas as pl
from jax.experimental.pallas import tpu as pltpu
from jax.sharding import PartitionSpec as P

HEADS = 16
HEAD = 64
PACK = 4
WIDE = PACK * HEAD
CHUNKS = 3
NEVER = -1e37
BF16 = jnp.bfloat16
F32 = jnp.float32
SCALE = math.log2(math.e) / math.sqrt(HEAD)
VMEM_LIMIT = 28 * 1024 * 1024
COST = 4000000000
EARLY_COST = 4000000000
NEAR_COST = 4000000000
ACROSS_COST = 4000000000


def lane_head(shape):
    return lax.broadcasted_iota(jnp.int32, shape, len(shape) - 1) // HEAD


def spread(packed):
    lane = lane_head((1, WIDE))
    return jnp.concatenate(
        [packed * (lane == h).astype(F32).astype(BF16) for h in range(PACK)], axis=0
    )


def gather_diagonal(full):
    lane = lane_head((HEAD, WIDE))
    total = full[:HEAD]
    for h in range(1, PACK):
        total = jnp.where(lane == h, full[h * HEAD : (h + 1) * HEAD], total)
    return total


def dot(a, b):
    return jnp.dot(a, b, preferred_element_type=F32)


def dot_nt(a, b):
    return lax.dot_general(a, b, (((1,), (1,)), ((), ())), preferred_element_type=F32)


def update(scores, values_t, carried):
    row_max, total, summed = carried
    new_max = jnp.maximum(row_max, jnp.max(scores, axis=0, keepdims=True))
    exponent = jnp.exp2((scores - new_max) * SCALE)
    factor = jnp.exp2((row_max - new_max) * SCALE)
    total = total * factor + jnp.sum(exponent, axis=0, keepdims=True)
    summed = summed * factor + gather_diagonal(dot(values_t, exponent.astype(BF16)))
    return new_max, total, summed


def halves(pair):
    lane = lax.broadcasted_iota(jnp.int32, pair.shape, 1)
    turned = pltpu.roll(pair, HEAD, 1)
    low = lane < HEAD
    zero = jnp.zeros_like(pair)
    first = (jnp.where(low, pair, zero), jnp.where(low, zero, turned))
    second = (jnp.where(low, turned, zero), jnp.where(low, zero, pair))
    return first, second


def widest_of(hw):
    best, where = hw[0], 0
    for c in range(1, hw.shape[0]):
        larger = hw[c] > best
        best = jnp.where(larger, hw[c], best)
        where = jnp.where(larger, c, where)
    return where


def project_values(wvt, tokens, g, blocks, rows):
    v = dot_nt(wvt[g * WIDE : (g + 1) * WIDE, :], tokens)
    parts = []
    for c in range(0, blocks, 2):
        for left, right in halves(v[:, c * rows : (c + 2) * rows]):
            parts.append((left.astype(BF16), right.astype(BF16)))
    return parts, v[:, blocks * rows :].astype(BF16)


def prepare_kernel(x, f0, f1, f2, sems):
    lon, lat, _ = x.shape
    span = lat * lon // sems.shape[0]
    out = (f0, f1, f2)
    count = f0.shape[0] // span // lon
    copies = []
    for j in range(CHUNKS):
        for c in range(count):
            for o in range(lon):
                at = (c * lon + o) * span
                copies.append(
                    pltpu.make_async_copy(
                        x.at[o, pl.ds((j * count + c) * span, span), :],
                        out[j].at[pl.ds(at, span), :],
                        sems.at[len(copies)],
                    )
                )
                copies[-1].start()
    for copy in copies:
        copy.wait()


def band_kernel(hw, x0, x1, x2, band):
    wide = widest_of(hw)
    rows = band.shape[0]
    per = x0.shape[0] // rows
    for c in range(CHUNKS * per):

        @pl.when(wide == c)
        def _(c=c):
            at = (c % per) * rows
            band[...] = (x0, x1, x2)[c // per][at : at + rows, :]


def own_kernel(x0, x1, x2, s, w, qc, keys, vals, wk, wvt, own, both, wq, wv, sems):
    lon, _, width = s.shape
    nlb, groups, rows, _ = keys.shape
    rows //= 2
    span = rows // lon
    fetch = []
    for which, place in ((1, wk), (0, wq), (2, wv)):
        for g in range(groups):
            fetch.append(
                pltpu.make_async_copy(
                    w.at[:, pl.ds(which * width + g * WIDE, WIDE)],
                    place.at[:, pl.ds(g * WIDE, WIDE)],
                    sems.at[len(fetch)],
                )
            )
            fetch[-1].start()
    at = 0
    for part in (x0, x1, x2):
        for c in range(part.shape[0] // rows):
            block = part[c * rows : (c + 1) * rows, :]
            own[at : at + rows, :] = block
            both[2 * at : 2 * at + rows, :] = block
            at += rows
    for c in range(nlb):
        for o in range(lon):
            at = (2 * c + 1) * rows + o * span
            both[at : at + span, :] = s[o, c * span : (c + 1) * span, :]
    for g in range(groups):
        fetch[g].wait()
        k = dot(both[...], wk[:, g * WIDE : (g + 1) * WIDE]).astype(BF16)
        for c in range(nlb):
            keys[c, g] = k[2 * c * rows : 2 * (c + 1) * rows, :]
    for g in range(groups):
        fetch[groups + g].wait()
        q = dot(own[...], wq[:, g * WIDE : (g + 1) * WIDE]).astype(BF16).astype(F32)
        for b in range(nlb):
            qt = q[b * rows : (b + 1) * rows, :].T
            qc[b * groups + g] = jnp.concatenate(
                [qt[h * HEAD : (h + 1) * HEAD, :] for h in range(PACK)], axis=1
            ).astype(BF16)
    for g in range(groups):
        fetch[2 * groups + g].wait()
        wvt[g * WIDE : (g + 1) * WIDE, :] = wv[:, g * WIDE : (g + 1) * WIDE].T
        v = dot_nt(wvt[g * WIDE : (g + 1) * WIDE, :], both[...]).astype(BF16)
        for c in range(nlb):
            vals[c, g] = v[:, 2 * c * rows : 2 * (c + 1) * rows]


def near_kernel(nbr, qc, keys, vals, m, l, acc):
    nlb, groups, _, _ = keys.shape
    for b in range(nlb):
        c0, c1 = nbr[b, 0], nbr[b, 1]
        for g in range(groups):
            t = b * groups + g
            k = jnp.concatenate([keys[c0, g], keys[c1, g]], axis=0)
            v = jnp.concatenate([vals[c0, g], vals[c1, g]], axis=1)
            scores = dot(k, spread(qc[t]))
            row_max = jnp.max(scores, axis=0, keepdims=True)
            exponent = jnp.exp2((scores - row_max) * SCALE)
            m[t] = row_max
            l[t] = jnp.sum(exponent, axis=0, keepdims=True)
            acc[t] = gather_diagonal(dot(v, exponent.astype(BF16)))


def project_far(tokens, w, wvt, keys, vals, wkeys, wvals):
    nlb, groups, rows, _ = keys.shape
    for g in range(groups):
        k = dot(tokens[...], w[:, g * WIDE : (g + 1) * WIDE]).astype(BF16)
        parts, rest = project_values(wvt, tokens[...], g, nlb, rows)
        for c in range(nlb):
            keys[c, g] = k[c * rows : (c + 1) * rows, :]
            vals[0, c, g] = parts[c][0]
            vals[1, c, g] = parts[c][1]
        if wkeys is not None:
            wkeys[g] = k[nlb * rows :, :]
            wvals[g] = rest


def attend_far(nbr, seen, wide, qc, pick_keys, pick_vals, wkeys, wvals, before, finish):
    nlb = nbr.shape[0]
    groups = qc.shape[0] // nlb
    for b in range(nlb):
        c0, c1 = nbr[b, 0], nbr[b, 1]
        for g in range(groups):
            t = b * groups + g
            q = spread(qc[t])
            ks = [pick_keys(c0, g), pick_keys(c1, g)]
            rows = ks[0].shape[0]
            v = pick_vals(0, c0, g) + pick_vals(1, c1, g)
            if wkeys is not None:
                ks.append(wkeys[g])
                v = jnp.concatenate([v, wvals[g]], axis=1)
            scores = dot(jnp.concatenate(ks, axis=0), q)
            pieces = [scores[:rows], scores[rows : 2 * rows]]
            if seen is not None:
                pieces[0] = jnp.where(seen[c0] >= 2, pieces[0], NEVER)
                pieces[1] = jnp.where(seen[c1] >= 2, pieces[1], NEVER)
            if wkeys is not None:
                member = (c0 == wide) | (c1 == wide)
                pieces.append(jnp.where(member, scores[2 * rows :], NEVER))
            scores = jnp.concatenate(pieces, axis=0)
            finish(b, g, *update(scores, v, tuple(r[t] for r in before)))


def from_one(keys, vals):
    return (lambda c, g: keys[c, g]), (lambda side, c, g: vals[side, c, g])


def from_two(keys, vals, more_keys, more_vals):
    first = keys.shape[0]

    def pick_keys(c, g):
        here, there = keys[jnp.minimum(c, first - 1), g], more_keys[jnp.maximum(c - first, 0), g]
        return jnp.where(c < first, here, there)

    def pick_vals(side, c, g):
        here = vals[side, jnp.minimum(c, first - 1), g]
        there = more_vals[side, jnp.maximum(c - first, 0), g]
        return jnp.where(c < first, here, there)

    return pick_keys, pick_vals


def keep(m, l, acc, groups):
    def store(b, g, row_max, total, summed):
        t = b * groups + g
        m[t], l[t], acc[t] = row_max, total, summed

    return store


def across_kernel(nbr, hw, f0, f1, f2, wf, wb, w, wvt, qc, m_in, l_in, acc_in,
                  m, l, acc, tokens, keys, vals, wkeys, wvals):
    at = 0
    for part in (f0, f1, f2, wf, wb):
        tokens[at : at + part.shape[0], :] = part[...]
        at += part.shape[0]
    project_far(tokens, w, wvt, keys, vals, wkeys, wvals)
    attend_far(nbr, hw, widest_of(hw), qc, *from_one(keys, vals), wkeys, wvals, (m_in, l_in, acc_in), keep(m, l, acc, keys.shape[1]))


def early_kernel(g0, g1, w, wvt, keys, vals, tokens):
    tokens[: g0.shape[0], :] = g0[...]
    tokens[g0.shape[0] :, :] = g1[...]
    project_far(tokens, w, wvt, keys, vals, None, None)


def onward_kernel(nbr, hw, g2, w, wvt, qc, early_keys, early_vals, m_in, l_in, acc_in, m, l, acc, keys, vals):
    project_far(g2, w, wvt, keys, vals, None, None)
    picks = from_two(early_keys, early_vals, keys, vals)
    store = keep(m, l, acc, keys.shape[1])
    attend_far(nbr, hw, None, qc, *picks, None, None, (m_in, l_in, acc_in), store)


def payload_kernel(hw, f0, f1, f2, g0, g1, g2, wf, wb, out):
    here = lax.axis_index("lon")
    wide = widest_of(hw)
    size = f0.shape[0]
    rows = wf.shape[0]
    per = size // rows
    base = CHUNKS * size

    def fill(sent, other, wide_sent):
        for j in range(CHUNKS):
            out[j * size : (j + 1) * size, :] = sent[j][...]
        out[base : base + rows, :] = wide_sent[...]
        for c in range(CHUNKS * per):

            @pl.when(wide == c)
            def _(c=c):
                at = (c % per) * rows
                out[base + rows :, :] = other[c // per][at : at + rows, :]

    kind = (here ^ (here >> 1)) & 1

    @pl.when(kind == 0)
    def _():
        fill((f0, f1, f2), (g0, g1, g2), wb)

    @pl.when(kind != 0)
    def _():
        fill((g0, g1, g2), (f0, f1, f2), wf)


def last_kernel(nbr, hw, e, w, wvt, wout, qc, m_in, l_in, acc_in, out, keys, vals, wkeys, wvals, attended):
    nlb, groups, rows, _ = keys.shape
    lon = out.shape[0]
    span = rows // lon

    def store(b, g, _, total, summed):
        done = (summed * (1.0 / total)).T
        attended[b * rows : (b + 1) * rows, g * WIDE : (g + 1) * WIDE] = jnp.concatenate(
            [done[h * HEAD : (h + 1) * HEAD, :] for h in range(PACK)], axis=1
        ).astype(BF16)

    project_far(e, w, wvt, keys, vals, wkeys, wvals)
    attend_far(nbr, None, widest_of(hw), qc, *from_one(keys, vals), wkeys, wvals, (m_in, l_in, acc_in), store)
    for g in range(groups):
        r = dot(attended[...], wout[:, g * WIDE : (g + 1) * WIDE]).astype(BF16)
        for b in range(nlb):
            for o in range(lon):
                at = b * rows + o * span
                out[o, b * span : (b + 1) * span, g * WIDE : (g + 1) * WIDE] = r[at : at + span, :]


def call(kernel, scalars, arrays, outs, scratch, unread=0, cost=COST):
    smem = pl.BlockSpec(memory_space=pltpu.SMEM)
    vmem = pl.BlockSpec(memory_space=pltpu.VMEM)
    single = not isinstance(outs, (list, tuple))
    specs = [vmem] * (len(arrays) - unread) + [pl.BlockSpec(memory_space=pltpu.HBM)] * unread
    read = len(arrays) - unread
    arrays = [
        a if i < read else pltpu.with_memory_space_constraint(a, pltpu.HBM)
        for i, a in enumerate(arrays)
    ]
    return pl.pallas_call(
        kernel,
        out_shape=outs,
        in_specs=[smem] * len(scalars) + specs,
        out_specs=vmem if single else [vmem] * len(outs),
        scratch_shapes=scratch,
        compiler_params=pltpu.CompilerParams(vmem_limit_bytes=VMEM_LIMIT),
        cost_estimate=pl.CostEstimate(flops=cost, bytes_accessed=1000, transcendentals=0),
    )(*scalars, *arrays)


def after(value, *others):
    return lax.optimization_barrier((value, *others))[0]


def per_device(tokens, projection, out_weight, half_width, neighbours):
    lon, lat, width = tokens.shape
    nlb = neighbours.shape[0]
    span = lat // nlb
    rows = lon * span
    groups = width // WIDE
    tiles = nlb * groups
    count = lax.axis_size("lon")
    devices = range(count)

    def permute(block, step):
        return lax.ppermute(block, "lon", [(i, step(i) % count) for i in devices])

    def sibling(i):
        return i ^ 1

    def across(i):
        return i ^ 2

    def onward(i):
        return i - 4 if i & 2 else i + 4

    def backward(i):
        return i + 4 if i & 2 else i - 4

    tile = (tiles, HEAD, WIDE)
    row = (tiles, 1, WIDE)
    carried_shapes = [
        jax.ShapeDtypeStruct(row, F32),
        jax.ShapeDtypeStruct(row, F32),
        jax.ShapeDtypeStruct(tile, F32),
    ]
    key_scratch = pltpu.VMEM((nlb, groups, rows, WIDE), BF16)
    val_scratch = pltpu.VMEM((2, nlb, groups, WIDE, 2 * rows), BF16)
    wide_scratch = [
        pltpu.VMEM((groups, 2 * rows, WIDE), BF16),
        pltpu.VMEM((groups, WIDE, 2 * rows), BF16),
    ]

    beside = permute(tokens, sibling)
    chunk = jax.ShapeDtypeStruct((nlb * rows // CHUNKS, width), BF16)
    parts = call(
        prepare_kernel, (), (tokens,), [chunk] * CHUNKS, [pltpu.SemaphoreType.DMA((nlb * lon,))], unread=1
    )
    f = [permute(part, across) for part in parts]
    band = call(
        band_kernel, (half_width,), tuple(parts), jax.ShapeDtypeStruct((rows, width), BF16), []
    )
    wf = permute(band, onward)
    wb = permute(band, backward)
    g0 = permute(f[0], onward)
    held, *_ = lax.optimization_barrier((parts[0], f[0]))
    qc, keys, vals, wk, wvt = call(
        own_kernel,
        (),
        (held, *parts[1:], beside, projection),
        [
            jax.ShapeDtypeStruct(tile, BF16),
            jax.ShapeDtypeStruct((nlb, groups, 2 * rows, WIDE), BF16),
            jax.ShapeDtypeStruct((nlb, groups, WIDE, 2 * rows), BF16),
            jax.ShapeDtypeStruct((width, width), BF16),
            jax.ShapeDtypeStruct((width, width), BF16),
        ],
        [
            pltpu.VMEM((nlb * rows, width), BF16),
            pltpu.VMEM((2 * nlb * rows, width), BF16),
            pltpu.VMEM((width, width), BF16),
            pltpu.VMEM((width, width), BF16),
            pltpu.SemaphoreType.DMA((3 * groups,)),
        ],
        unread=1,
    )
    g1 = permute(after(f[1], qc), onward)
    m, l, acc = call(
        near_kernel,
        (neighbours,),
        (after(qc, f[1]), keys, vals),
        carried_shapes,
        [],
        cost=NEAR_COST,
    )
    g2 = permute(after(f[2], m), onward)
    m, l, acc = call(
        across_kernel,
        (neighbours, half_width),
        (*f, wf, wb, wk, wvt, qc, m, l, acc),
        carried_shapes,
        [pltpu.VMEM(((nlb + 2) * rows, width), BF16), key_scratch, val_scratch, *wide_scratch],
        cost=ACROSS_COST,
    )
    early = nlb // CHUNKS * (CHUNKS - 1)
    early_keys, early_vals = call(
        early_kernel,
        (),
        (after(g0, m), g1, wk, wvt),
        [
            jax.ShapeDtypeStruct((early, groups, rows, WIDE), BF16),
            jax.ShapeDtypeStruct((2, early, groups, WIDE, 2 * rows), BF16),
        ],
        [pltpu.VMEM((early * rows, width), BF16)],
        cost=EARLY_COST,
    )
    e = call(
        payload_kernel,
        (half_width,),
        (*f, g0, g1, g2, after(wf, early_keys), wb),
        jax.ShapeDtypeStruct(((nlb + 2) * rows, width), BF16),
        [],
    )
    e = permute(e, sibling)
    m, l, acc = call(
        onward_kernel,
        (neighbours, half_width),
        (g2, wk, wvt, qc, early_keys, early_vals, m, l, acc),
        carried_shapes,
        [
            pltpu.VMEM((nlb - early, groups, rows, WIDE), BF16),
            pltpu.VMEM((2, nlb - early, groups, WIDE, 2 * rows), BF16),
        ],
    )
    return call(
        last_kernel,
        (neighbours, half_width),
        (e, wk, wvt, out_weight, qc, m, l, acc),
        jax.ShapeDtypeStruct(tokens.shape, BF16),
        [
            key_scratch,
            val_scratch,
            *wide_scratch,
            pltpu.VMEM((nlb * rows, width), BF16),
        ],
    )


def solution(mesh):
    return jax.shard_map(
        per_device,
        mesh=mesh,
        in_specs=(P(("groups", "lon"), None, None), P(), P(), P(), P()),
        out_specs=P(("groups", "lon"), None, None),
        check_vma=False,
    )
```

```python
import math

import jax
import jax.numpy as jnp
from jax import lax
from jax.experimental import pallas as pl
from jax.experimental.pallas import tpu as pltpu
from jax.sharding import PartitionSpec as P

HEADS = 16
HEAD = 64
PACK = 4
WIDE = PACK * HEAD
CHUNKS = 3
NEVER = -1e37
BF16 = jnp.bfloat16
F32 = jnp.float32
SCALE = math.log2(math.e) / math.sqrt(HEAD)
VMEM_LIMIT = 28 * 1024 * 1024
COST = 2000000000
EARLY_COST = 4000000000
NEAR_COST = 2000000000
ACROSS_COST = 2000000000


def lane_head(shape):
    return lax.broadcasted_iota(jnp.int32, shape, len(shape) - 1) // HEAD


def spread(packed):
    lane = lane_head((1, WIDE))
    return jnp.concatenate(
        [packed * (lane == h).astype(F32).astype(BF16) for h in range(PACK)], axis=0
    )


def gather_diagonal(full):
    lane = lane_head((HEAD, WIDE))
    total = full[:HEAD]
    for h in range(1, PACK):
        total = jnp.where(lane == h, full[h * HEAD : (h + 1) * HEAD], total)
    return total


def dot(a, b):
    return jnp.dot(a, b, preferred_element_type=F32)


def dot_nt(a, b):
    return lax.dot_general(a, b, (((1,), (1,)), ((), ())), preferred_element_type=F32)


def update(scores, values_t, carried):
    row_max, total, summed = carried
    new_max = jnp.maximum(row_max, jnp.max(scores, axis=0, keepdims=True))
    exponent = jnp.exp2((scores - new_max) * SCALE)
    factor = jnp.exp2((row_max - new_max) * SCALE)
    total = total * factor + jnp.sum(exponent, axis=0, keepdims=True)
    summed = summed * factor + gather_diagonal(dot(values_t, exponent.astype(BF16)))
    return new_max, total, summed


def halves(pair):
    lane = lax.broadcasted_iota(jnp.int32, pair.shape, 1)
    turned = pltpu.roll(pair, HEAD, 1)
    low = lane < HEAD
    zero = jnp.zeros_like(pair)
    first = (jnp.where(low, pair, zero), jnp.where(low, zero, turned))
    second = (jnp.where(low, turned, zero), jnp.where(low, zero, pair))
    return first, second


def widest_of(hw):
    best, where = hw[0], 0
    for c in range(1, hw.shape[0]):
        larger = hw[c] > best
        best = jnp.where(larger, hw[c], best)
        where = jnp.where(larger, c, where)
    return where


def project_values(wvt, tokens, g, blocks, rows):
    v = dot_nt(wvt[g * WIDE : (g + 1) * WIDE, :], tokens)
    parts = []
    for c in range(0, blocks, 2):
        for left, right in halves(v[:, c * rows : (c + 2) * rows]):
            parts.append((left.astype(BF16), right.astype(BF16)))
    return parts, v[:, blocks * rows :].astype(BF16)


def prepare_kernel(x, f0, f1, f2, sems):
    lon, lat, _ = x.shape
    span = lat * lon // sems.shape[0]
    out = (f0, f1, f2)
    count = f0.shape[0] // span // lon
    copies = []
    for j in range(CHUNKS):
        for c in range(count):
            for o in range(lon):
                at = (c * lon + o) * span
                copies.append(
                    pltpu.make_async_copy(
                        x.at[o, pl.ds((j * count + c) * span, span), :],
                        out[j].at[pl.ds(at, span), :],
                        sems.at[len(copies)],
                    )
                )
                copies[-1].start()
    for copy in copies:
        copy.wait()


def band_kernel(hw, x0, x1, x2, s, bands):
    wide = widest_of(hw)
    lon = s.shape[0]
    rows = bands.shape[0] // 2
    span = rows // lon
    per = x0.shape[0] // rows
    for c in range(CHUNKS * per):

        @pl.when(wide == c)
        def _(c=c):
            at = (c % per) * rows
            bands[:rows, :] = (x0, x1, x2)[c // per][at : at + rows, :]
            for o in range(lon):
                bands[rows + o * span : rows + (o + 1) * span, :] = s[o, c * span : (c + 1) * span, :]


def own_kernel(x0, x1, x2, s, w, qc, keys, vals, wvt, own, both):
    lon, _, width = s.shape
    nlb, groups, rows, _ = keys.shape
    rows //= 2
    span = rows // lon
    at = 0
    for part in (x0, x1, x2):
        for c in range(part.shape[0] // rows):
            block = part[c * rows : (c + 1) * rows, :]
            own[at : at + rows, :] = block
            both[2 * at : 2 * at + rows, :] = block
            at += rows
    for c in range(nlb):
        for o in range(lon):
            at = (2 * c + 1) * rows + o * span
            both[at : at + span, :] = s[o, c * span : (c + 1) * span, :]
    for g in range(groups):
        k = dot(both[...], w[:, width + g * WIDE : width + (g + 1) * WIDE]).astype(BF16)
        for c in range(nlb):
            keys[c, g] = k[2 * c * rows : 2 * (c + 1) * rows, :]
        q = dot(own[...], w[:, g * WIDE : (g + 1) * WIDE]).astype(BF16).astype(F32)
        for b in range(nlb):
            qt = q[b * rows : (b + 1) * rows, :].T
            qc[b * groups + g] = jnp.concatenate(
                [qt[h * HEAD : (h + 1) * HEAD, :] for h in range(PACK)], axis=1
            ).astype(BF16)
        at = 2 * width + g * WIDE
        wvt[g * WIDE : (g + 1) * WIDE, :] = w[:, at : at + WIDE].T
        v = dot_nt(wvt[g * WIDE : (g + 1) * WIDE, :], both[...]).astype(BF16)
        for c in range(nlb):
            vals[c, g] = v[:, 2 * c * rows : 2 * (c + 1) * rows]


def near_kernel(nbr, qc, keys, vals, m, l, acc):
    nlb, groups, _, _ = keys.shape
    for b in range(nlb):
        c0, c1 = nbr[b, 0], nbr[b, 1]
        for g in range(groups):
            t = b * groups + g
            k = jnp.concatenate([keys[c0, g], keys[c1, g]], axis=0)
            v = jnp.concatenate([vals[c0, g], vals[c1, g]], axis=1)
            scores = dot(k, spread(qc[t]))
            row_max = jnp.max(scores, axis=0, keepdims=True)
            exponent = jnp.exp2((scores - row_max) * SCALE)
            m[t] = row_max
            l[t] = jnp.sum(exponent, axis=0, keepdims=True)
            acc[t] = gather_diagonal(dot(v, exponent.astype(BF16)))


def project_far(tokens, w, wvt, keys, vals, wkeys, wvals):
    nlb, groups, rows, _ = keys.shape
    width = tokens.shape[1]
    for g in range(groups):
        k = dot(tokens[...], w[:, width + g * WIDE : width + (g + 1) * WIDE]).astype(BF16)
        parts, rest = project_values(wvt, tokens[...], g, nlb, rows)
        for c in range(nlb):
            keys[c, g] = k[c * rows : (c + 1) * rows, :]
            vals[0, c, g] = parts[c][0]
            vals[1, c, g] = parts[c][1]
        if wkeys is not None:
            wkeys[g] = k[nlb * rows :, :]
            wvals[g] = rest


def attend_far(nbr, seen, wide, qc, pick_keys, pick_vals, wkeys, wvals, before, finish):
    nlb = nbr.shape[0]
    groups = qc.shape[0] // nlb
    for b in range(nlb):
        c0, c1 = nbr[b, 0], nbr[b, 1]
        for g in range(groups):
            t = b * groups + g
            q = spread(qc[t])
            ks = [pick_keys(c0, g), pick_keys(c1, g)]
            rows = ks[0].shape[0]
            v = pick_vals(0, c0, g) + pick_vals(1, c1, g)
            if wkeys is not None:
                ks.append(wkeys[g])
                v = jnp.concatenate([v, wvals[g]], axis=1)
            scores = dot(jnp.concatenate(ks, axis=0), q)
            pieces = [scores[:rows], scores[rows : 2 * rows]]
            if seen is not None:
                pieces[0] = jnp.where(seen[c0] >= 2, pieces[0], NEVER)
                pieces[1] = jnp.where(seen[c1] >= 2, pieces[1], NEVER)
            if wkeys is not None:
                member = (c0 == wide) | (c1 == wide)
                pieces.append(jnp.where(member, scores[2 * rows :], NEVER))
            scores = jnp.concatenate(pieces, axis=0)
            finish(b, g, *update(scores, v, tuple(r[t] for r in before)))


def from_one(keys, vals):
    return (lambda c, g: keys[c, g]), (lambda side, c, g: vals[side, c, g])


def from_two(keys, vals, more_keys, more_vals):
    first = keys.shape[0]

    def pick_keys(c, g):
        here, there = keys[jnp.minimum(c, first - 1), g], more_keys[jnp.maximum(c - first, 0), g]
        return jnp.where(c < first, here, there)

    def pick_vals(side, c, g):
        here = vals[side, jnp.minimum(c, first - 1), g]
        there = more_vals[side, jnp.maximum(c - first, 0), g]
        return jnp.where(c < first, here, there)

    return pick_keys, pick_vals


def keep(m, l, acc, groups):
    def store(b, g, row_max, total, summed):
        t = b * groups + g
        m[t], l[t], acc[t] = row_max, total, summed

    return store


def across_kernel(nbr, hw, f0, f1, f2, bands, w, wvt, qc, m_in, l_in, acc_in,
                  m, l, acc, tokens, keys, vals, wkeys, wvals):
    at = 0
    for part in (f0, f1, f2, bands):
        tokens[at : at + part.shape[0], :] = part[...]
        at += part.shape[0]
    project_far(tokens, w, wvt, keys, vals, wkeys, wvals)
    attend_far(nbr, hw, widest_of(hw), qc, *from_one(keys, vals), wkeys, wvals, (m_in, l_in, acc_in), keep(m, l, acc, keys.shape[1]))


def early_kernel(g0, g1, w, wvt, keys, vals, tokens):
    tokens[: g0.shape[0], :] = g0[...]
    tokens[g0.shape[0] :, :] = g1[...]
    project_far(tokens, w, wvt, keys, vals, None, None)


def onward_kernel(nbr, hw, g2, w, wvt, qc, early_keys, early_vals, m_in, l_in, acc_in, m, l, acc, keys, vals):
    project_far(g2, w, wvt, keys, vals, None, None)
    picks = from_two(early_keys, early_vals, keys, vals)
    store = keep(m, l, acc, keys.shape[1])
    attend_far(nbr, hw, None, qc, *picks, None, None, (m_in, l_in, acc_in), store)


def payload_kernel(hw, f0, f1, f2, g0, g1, g2, bands, out):
    here = lax.axis_index("lon")
    wide = widest_of(hw)
    size = f0.shape[0]
    rows = bands.shape[0] // 2
    per = size // rows
    base = CHUNKS * size

    def fill(sent, other):
        for j in range(CHUNKS):
            out[j * size : (j + 1) * size, :] = sent[j][...]
        out[base : base + rows, :] = bands[rows:, :]
        for c in range(CHUNKS * per):

            @pl.when(wide == c)
            def _(c=c):
                at = (c % per) * rows
                out[base + rows :, :] = other[c // per][at : at + rows, :]

    kind = (here ^ (here >> 1)) & 1

    @pl.when(kind == 0)
    def _():
        fill((f0, f1, f2), (g0, g1, g2))

    @pl.when(kind != 0)
    def _():
        fill((g0, g1, g2), (f0, f1, f2))


def last_kernel(nbr, hw, e, w, wvt, wout, qc, m_in, l_in, acc_in, out, keys, vals, wkeys, wvals, attended):
    nlb, groups, rows, _ = keys.shape
    lon = out.shape[0]
    span = rows // lon

    def store(b, g, _, total, summed):
        done = (summed * (1.0 / total)).T
        attended[b * rows : (b + 1) * rows, g * WIDE : (g + 1) * WIDE] = jnp.concatenate(
            [done[h * HEAD : (h + 1) * HEAD, :] for h in range(PACK)], axis=1
        ).astype(BF16)

    project_far(e, w, wvt, keys, vals, wkeys, wvals)
    attend_far(nbr, None, widest_of(hw), qc, *from_one(keys, vals), wkeys, wvals, (m_in, l_in, acc_in), store)
    for g in range(groups):
        r = dot(attended[...], wout[:, g * WIDE : (g + 1) * WIDE]).astype(BF16)
        for b in range(nlb):
            for o in range(lon):
                at = b * rows + o * span
                out[o, b * span : (b + 1) * span, g * WIDE : (g + 1) * WIDE] = r[at : at + span, :]


def call(kernel, scalars, arrays, outs, scratch, unread=0, cost=COST):
    smem = pl.BlockSpec(memory_space=pltpu.SMEM)
    vmem = pl.BlockSpec(memory_space=pltpu.VMEM)
    single = not isinstance(outs, (list, tuple))
    specs = [vmem] * (len(arrays) - unread) + [pl.BlockSpec(memory_space=pltpu.HBM)] * unread
    read = len(arrays) - unread
    arrays = [
        a if i < read else pltpu.with_memory_space_constraint(a, pltpu.HBM)
        for i, a in enumerate(arrays)
    ]
    return pl.pallas_call(
        kernel,
        out_shape=outs,
        in_specs=[smem] * len(scalars) + specs,
        out_specs=vmem if single else [vmem] * len(outs),
        scratch_shapes=scratch,
        compiler_params=pltpu.CompilerParams(vmem_limit_bytes=VMEM_LIMIT),
        cost_estimate=pl.CostEstimate(flops=cost, bytes_accessed=1000, transcendentals=0),
    )(*scalars, *arrays)


def after(value, *others):
    return lax.optimization_barrier((value, *others))[0]


def per_device(tokens, projection, out_weight, half_width, neighbours):
    lon, lat, width = tokens.shape
    nlb = neighbours.shape[0]
    span = lat // nlb
    rows = lon * span
    groups = width // WIDE
    tiles = nlb * groups
    count = lax.axis_size("lon")
    devices = range(count)

    def permute(block, step):
        return lax.ppermute(block, "lon", [(i, step(i) % count) for i in devices])

    def sibling(i):
        return i ^ 1

    def across(i):
        return i ^ 2

    def onward(i):
        return i - 4 if i & 2 else i + 4

    def outward(i):
        return i - 4 if i & 1 else i + 4

    tile = (tiles, HEAD, WIDE)
    row = (tiles, 1, WIDE)
    carried_shapes = [
        jax.ShapeDtypeStruct(row, F32),
        jax.ShapeDtypeStruct(row, F32),
        jax.ShapeDtypeStruct(tile, F32),
    ]
    key_scratch = pltpu.VMEM((nlb, groups, rows, WIDE), BF16)
    val_scratch = pltpu.VMEM((2, nlb, groups, WIDE, 2 * rows), BF16)
    wide_scratch = [
        pltpu.VMEM((groups, 2 * rows, WIDE), BF16),
        pltpu.VMEM((groups, WIDE, 2 * rows), BF16),
    ]

    beside = permute(tokens, sibling)
    chunk = jax.ShapeDtypeStruct((nlb * rows // CHUNKS, width), BF16)
    parts = call(
        prepare_kernel, (), (tokens,), [chunk] * CHUNKS, [pltpu.SemaphoreType.DMA((nlb * lon,))], unread=1
    )
    f = [permute(part, across) for part in parts]
    bands = call(
        band_kernel, (half_width,), (*parts, beside), jax.ShapeDtypeStruct((2 * rows, width), BF16), []
    )
    bands = permute(bands, outward)
    g0 = permute(f[0], onward)
    held, *_ = lax.optimization_barrier((parts[0], f[0]))
    qc, keys, vals, wvt = call(
        own_kernel,
        (),
        (held, *parts[1:], beside, projection),
        [
            jax.ShapeDtypeStruct(tile, BF16),
            jax.ShapeDtypeStruct((nlb, groups, 2 * rows, WIDE), BF16),
            jax.ShapeDtypeStruct((nlb, groups, WIDE, 2 * rows), BF16),
            jax.ShapeDtypeStruct((width, width), BF16),
        ],
        [pltpu.VMEM((nlb * rows, width), BF16), pltpu.VMEM((2 * nlb * rows, width), BF16)],
    )
    g1 = permute(after(f[1], qc), onward)
    m, l, acc = call(
        near_kernel,
        (neighbours,),
        (after(qc, f[1], bands), keys, vals),
        carried_shapes,
        [],
        cost=NEAR_COST,
    )
    g2 = permute(after(f[2], m), onward)
    m, l, acc = call(
        across_kernel,
        (neighbours, half_width),
        (*f, bands, projection, wvt, qc, m, l, acc),
        carried_shapes,
        [pltpu.VMEM(((nlb + 2) * rows, width), BF16), key_scratch, val_scratch, *wide_scratch],
        cost=ACROSS_COST,
    )
    early = nlb // CHUNKS * (CHUNKS - 1)
    early_keys, early_vals = call(
        early_kernel,
        (),
        (after(g0, m), g1, projection, wvt),
        [
            jax.ShapeDtypeStruct((early, groups, rows, WIDE), BF16),
            jax.ShapeDtypeStruct((2, early, groups, WIDE, 2 * rows), BF16),
        ],
        [pltpu.VMEM((early * rows, width), BF16)],
        cost=EARLY_COST,
    )
    e = call(
        payload_kernel,
        (half_width,),
        (*f, g0, g1, g2, after(bands, early_keys)),
        jax.ShapeDtypeStruct(((nlb + 2) * rows, width), BF16),
        [],
    )
    e = permute(e, sibling)
    m, l, acc = call(
        onward_kernel,
        (neighbours, half_width),
        (g2, projection, wvt, qc, early_keys, early_vals, m, l, acc),
        carried_shapes,
        [
            pltpu.VMEM((nlb - early, groups, rows, WIDE), BF16),
            pltpu.VMEM((2, nlb - early, groups, WIDE, 2 * rows), BF16),
        ],
    )
    return call(
        last_kernel,
        (neighbours, half_width),
        (e, projection, wvt, out_weight, qc, m, l, acc),
        jax.ShapeDtypeStruct(tokens.shape, BF16),
        [
            key_scratch,
            val_scratch,
            *wide_scratch,
            pltpu.VMEM((nlb * rows, width), BF16),
        ],
    )


def solution(mesh):
    return jax.shard_map(
        per_device,
        mesh=mesh,
        in_specs=(P(("groups", "lon"), None, None), P(), P(), P(), P()),
        out_specs=P(("groups", "lon"), None, None),
        check_vma=False,
    )
```

```python
import math

import jax
import jax.numpy as jnp
from jax import lax
from jax.experimental import pallas as pl
from jax.experimental.pallas import tpu as pltpu
from jax.sharding import PartitionSpec as P

HEADS = 16
HEAD = 64
PACK = 4
WIDE = PACK * HEAD
CHUNKS = 3
NEVER = -1e37
BF16 = jnp.bfloat16
F32 = jnp.float32
SCALE = math.log2(math.e) / math.sqrt(HEAD)
MIB = 1024 * 1024
COST = 2000000000
EARLY_COST = 4000000000
NEAR_COST = 2000000000
ACROSS_COST = 2000000000


def lane_head(shape):
    return lax.broadcasted_iota(jnp.int32, shape, len(shape) - 1) // HEAD


def spread(packed):
    lane = lane_head((1, WIDE))
    return jnp.concatenate(
        [packed * (lane == h).astype(F32).astype(BF16) for h in range(PACK)], axis=0
    )


def gather_diagonal(full):
    lane = lane_head((HEAD, WIDE))
    total = full[:HEAD]
    for h in range(1, PACK):
        total = jnp.where(lane == h, full[h * HEAD : (h + 1) * HEAD], total)
    return total


def dot(a, b):
    return jnp.dot(a, b, preferred_element_type=F32)


def dot_nt(a, b):
    return lax.dot_general(a, b, (((1,), (1,)), ((), ())), preferred_element_type=F32)


def update(scores, values_t, carried):
    row_max, total, summed = carried
    new_max = jnp.maximum(row_max, jnp.max(scores, axis=0, keepdims=True))
    exponent = jnp.exp2((scores - new_max) * SCALE)
    factor = jnp.exp2((row_max - new_max) * SCALE)
    total = total * factor + jnp.sum(exponent, axis=0, keepdims=True)
    summed = summed * factor + gather_diagonal(dot(values_t, exponent.astype(BF16)))
    return new_max, total, summed


def halves(pair):
    lane = lax.broadcasted_iota(jnp.int32, pair.shape, 1)
    turned = pltpu.roll(pair, HEAD, 1)
    low = lane < HEAD
    zero = jnp.zeros_like(pair)
    first = (jnp.where(low, pair, zero), jnp.where(low, zero, turned))
    second = (jnp.where(low, turned, zero), jnp.where(low, zero, pair))
    return first, second


def widest_of(hw):
    best, where = hw[0], 0
    for c in range(1, hw.shape[0]):
        larger = hw[c] > best
        best = jnp.where(larger, hw[c], best)
        where = jnp.where(larger, c, where)
    return where


def project_values(wvt, tokens, g, blocks, rows):
    v = dot_nt(wvt[g * WIDE : (g + 1) * WIDE, :], tokens)
    parts = []
    for c in range(0, blocks, 2):
        for left, right in halves(v[:, c * rows : (c + 2) * rows]):
            parts.append((left.astype(BF16), right.astype(BF16)))
    return parts, v[:, blocks * rows :].astype(BF16)


def prepare_kernel(x, f0, f1, f2, sems):
    lon, lat, _ = x.shape
    span = lat * lon // sems.shape[0]
    out = (f0, f1, f2)
    count = f0.shape[0] // span // lon
    copies = []
    for j in range(CHUNKS):
        for c in range(count):
            for o in range(lon):
                at = (c * lon + o) * span
                copies.append(
                    pltpu.make_async_copy(
                        x.at[o, pl.ds((j * count + c) * span, span), :],
                        out[j].at[pl.ds(at, span), :],
                        sems.at[len(copies)],
                    )
                )
                copies[-1].start()
    for copy in copies:
        copy.wait()


def band_kernel(hw, x0, x1, x2, s, bands):
    wide = widest_of(hw)
    lon = s.shape[0]
    rows = bands.shape[0] // 2
    span = rows // lon
    per = x0.shape[0] // rows
    for c in range(CHUNKS * per):

        @pl.when(wide == c)
        def _(c=c):
            at = (c % per) * rows
            bands[:rows, :] = (x0, x1, x2)[c // per][at : at + rows, :]
            for o in range(lon):
                bands[rows + o * span : rows + (o + 1) * span, :] = s[o, c * span : (c + 1) * span, :]


def own_kernel(x0, x1, x2, s, w, qc, keys, vals, wvt, own, both):
    lon, _, width = s.shape
    nlb, groups, rows, _ = keys.shape
    rows //= 2
    span = rows // lon
    at = 0
    for part in (x0, x1, x2):
        for c in range(part.shape[0] // rows):
            block = part[c * rows : (c + 1) * rows, :]
            own[at : at + rows, :] = block
            both[2 * at : 2 * at + rows, :] = block
            at += rows
    for c in range(nlb):
        for o in range(lon):
            at = (2 * c + 1) * rows + o * span
            both[at : at + span, :] = s[o, c * span : (c + 1) * span, :]
    for g in range(groups):
        k = dot(both[...], w[:, width + g * WIDE : width + (g + 1) * WIDE]).astype(BF16)
        for c in range(nlb):
            keys[c, g] = k[2 * c * rows : 2 * (c + 1) * rows, :]
        q = dot(own[...], w[:, g * WIDE : (g + 1) * WIDE]).astype(BF16).astype(F32)
        for b in range(nlb):
            qt = q[b * rows : (b + 1) * rows, :].T
            qc[b * groups + g] = jnp.concatenate(
                [qt[h * HEAD : (h + 1) * HEAD, :] for h in range(PACK)], axis=1
            ).astype(BF16)
        at = 2 * width + g * WIDE
        wvt[g * WIDE : (g + 1) * WIDE, :] = w[:, at : at + WIDE].T
        v = dot_nt(wvt[g * WIDE : (g + 1) * WIDE, :], both[...]).astype(BF16)
        for c in range(nlb):
            vals[c, g] = v[:, 2 * c * rows : 2 * (c + 1) * rows]


def near_kernel(nbr, qc, keys, vals, m, l, acc):
    nlb, groups, _, _ = keys.shape
    for b in range(nlb):
        c0, c1 = nbr[b, 0], nbr[b, 1]
        for g in range(groups):
            t = b * groups + g
            k = jnp.concatenate([keys[c0, g], keys[c1, g]], axis=0)
            v = jnp.concatenate([vals[c0, g], vals[c1, g]], axis=1)
            scores = dot(k, spread(qc[t]))
            row_max = jnp.max(scores, axis=0, keepdims=True)
            exponent = jnp.exp2((scores - row_max) * SCALE)
            m[t] = row_max
            l[t] = jnp.sum(exponent, axis=0, keepdims=True)
            acc[t] = gather_diagonal(dot(v, exponent.astype(BF16)))


def project_far(tokens, w, wvt, keys, vals, wkeys, wvals):
    nlb, groups, rows, _ = keys.shape
    width = tokens.shape[1]
    ks = [
        dot(tokens[...], w[:, width + g * WIDE : width + (g + 1) * WIDE]).astype(BF16)
        for g in range(groups)
    ]
    for g in range(groups):
        k = ks[g]
        parts, rest = project_values(wvt, tokens[...], g, nlb, rows)
        for c in range(nlb):
            keys[c, g] = k[c * rows : (c + 1) * rows, :]
            vals[0, c, g] = parts[c][0]
            vals[1, c, g] = parts[c][1]
        if wkeys is not None:
            wkeys[g] = k[nlb * rows :, :]
            wvals[g] = rest


def attend_far(nbr, seen, wide, qc, keys, vals, wkeys, wvals, before, finish):
    nlb = nbr.shape[0]
    groups = qc.shape[0] // nlb
    for b in range(nlb):
        c0, c1 = nbr[b, 0], nbr[b, 1]
        for g in range(groups):
            t = b * groups + g
            q = spread(qc[t])
            ks = [keys[c0, g], keys[c1, g]]
            rows = ks[0].shape[0]
            v = vals[0, c0, g] + vals[1, c1, g]
            if wkeys is None:
                ks = ks + ks
            if wkeys is not None:
                ks.append(wkeys[g])
                v = jnp.concatenate([v, wvals[g]], axis=1)
            scores = dot(jnp.concatenate(ks, axis=0), q)
            pieces = [scores[:rows], scores[rows : 2 * rows]]
            if seen is not None:
                pieces[0] += jnp.where(seen[c0] >= 2, 0.0, NEVER)
                pieces[1] += jnp.where(seen[c1] >= 2, 0.0, NEVER)
            if wkeys is not None:
                member = (c0 == wide) | (c1 == wide)
                pieces.append(scores[2 * rows :] + jnp.where(member, 0.0, NEVER))
            scores = jnp.concatenate(pieces, axis=0)
            finish(b, g, *update(scores, v, tuple(r[t] for r in before)))


def keep(m, l, acc, groups):
    def store(b, g, row_max, total, summed):
        t = b * groups + g
        m[t], l[t], acc[t] = row_max, total, summed

    return store


def across_kernel(nbr, hw, f0, f1, f2, bands, w, wvt, qc, m_in, l_in, acc_in,
                  m, l, acc, tokens, keys, vals, wkeys, wvals):
    at = 0
    for part in (f0, f1, f2, bands):
        tokens[at : at + part.shape[0], :] = part[...]
        at += part.shape[0]
    project_far(tokens, w, wvt, keys, vals, wkeys, wvals)
    attend_far(nbr, hw, widest_of(hw), qc, keys, vals, wkeys, wvals, (m_in, l_in, acc_in), keep(m, l, acc, keys.shape[1]))


def early_kernel(g0, g1, w, wvt, keys, vals, tokens):
    tokens[: g0.shape[0], :] = g0[...]
    tokens[g0.shape[0] :, :] = g1[...]
    project_far(tokens, w, wvt, keys, vals, None, None)


def onward_kernel(nbr, hw, g2, w, wvt, qc, early_keys, early_vals, m_in, l_in, acc_in, m, l, acc, keys, vals):
    early = early_keys.shape[0]
    keys[:early] = early_keys[...]
    vals[:, :early] = early_vals[...]
    project_far(g2, w, wvt, keys.at[early:], vals.at[:, early:], None, None)
    store = keep(m, l, acc, keys.shape[1])
    attend_far(nbr, hw, None, qc, keys, vals, None, None, (m_in, l_in, acc_in), store)


def payload_kernel(hw, f0, f1, f2, g0, g1, g2, bands, out):
    here = lax.axis_index("lon")
    wide = widest_of(hw)
    size = f0.shape[0]
    rows = bands.shape[0] // 2
    per = size // rows
    base = CHUNKS * size

    def fill(sent, other):
        for j in range(CHUNKS):
            out[j * size : (j + 1) * size, :] = sent[j][...]
        out[base : base + rows, :] = bands[rows:, :]
        for c in range(CHUNKS * per):

            @pl.when(wide == c)
            def _(c=c):
                at = (c % per) * rows
                out[base + rows :, :] = other[c // per][at : at + rows, :]

    kind = (here ^ (here >> 1)) & 1

    @pl.when(kind == 0)
    def _():
        fill((f0, f1, f2), (g0, g1, g2))

    @pl.when(kind != 0)
    def _():
        fill((g0, g1, g2), (f0, f1, f2))


def last_kernel(nbr, hw, e, w, wvt, wout, qc, m_in, l_in, acc_in, out, keys, vals, wkeys, wvals, attended):
    nlb, groups, rows, _ = keys.shape
    lon = out.shape[0]
    span = rows // lon

    def store(b, g, _, total, summed):
        done = (summed * (1.0 / total)).T
        attended[b * rows : (b + 1) * rows, g * WIDE : (g + 1) * WIDE] = jnp.concatenate(
            [done[h * HEAD : (h + 1) * HEAD, :] for h in range(PACK)], axis=1
        ).astype(BF16)

    project_far(e, w, wvt, keys, vals, wkeys, wvals)
    attend_far(nbr, None, widest_of(hw), qc, keys, vals, wkeys, wvals, (m_in, l_in, acc_in), store)
    for g in range(groups):
        r = dot(attended[...], wout[:, g * WIDE : (g + 1) * WIDE]).astype(BF16)
        for b in range(nlb):
            for o in range(lon):
                at = b * rows + o * span
                out[o, b * span : (b + 1) * span, g * WIDE : (g + 1) * WIDE] = r[at : at + span, :]


def call(kernel, scalars, arrays, outs, scratch, unread=0, cost=COST, room=22):
    smem = pl.BlockSpec(memory_space=pltpu.SMEM)
    vmem = pl.BlockSpec(memory_space=pltpu.VMEM)
    single = not isinstance(outs, (list, tuple))
    specs = [vmem] * (len(arrays) - unread) + [pl.BlockSpec(memory_space=pltpu.HBM)] * unread
    read = len(arrays) - unread
    arrays = [
        a if i < read else pltpu.with_memory_space_constraint(a, pltpu.HBM)
        for i, a in enumerate(arrays)
    ]
    return pl.pallas_call(
        kernel,
        out_shape=outs,
        in_specs=[smem] * len(scalars) + specs,
        out_specs=vmem if single else [vmem] * len(outs),
        scratch_shapes=scratch,
        compiler_params=pltpu.CompilerParams(vmem_limit_bytes=room * MIB),
        cost_estimate=pl.CostEstimate(flops=cost, bytes_accessed=1000, transcendentals=0),
    )(*scalars, *arrays)


def after(value, *others):
    return lax.optimization_barrier((value, *others))[0]


def per_device(tokens, projection, out_weight, half_width, neighbours):
    lon, lat, width = tokens.shape
    nlb = neighbours.shape[0]
    span = lat // nlb
    rows = lon * span
    groups = width // WIDE
    tiles = nlb * groups
    count = lax.axis_size("lon")
    devices = range(count)

    def permute(block, step):
        return lax.ppermute(block, "lon", [(i, step(i) % count) for i in devices])

    def sibling(i):
        return i ^ 1

    def across(i):
        return i ^ 2

    def onward(i):
        return i - 4 if i & 2 else i + 4

    def outward(i):
        return i - 4 if i & 1 else i + 4

    tile = (tiles, HEAD, WIDE)
    row = (tiles, 1, WIDE)
    carried_shapes = [
        jax.ShapeDtypeStruct(row, F32),
        jax.ShapeDtypeStruct(row, F32),
        jax.ShapeDtypeStruct(tile, F32),
    ]
    key_scratch = pltpu.VMEM((nlb, groups, rows, WIDE), BF16)
    val_scratch = pltpu.VMEM((2, nlb, groups, WIDE, 2 * rows), BF16)
    wide_scratch = [
        pltpu.VMEM((groups, 2 * rows, WIDE), BF16),
        pltpu.VMEM((groups, WIDE, 2 * rows), BF16),
    ]

    beside = permute(tokens, sibling)
    chunk = jax.ShapeDtypeStruct((nlb * rows // CHUNKS, width), BF16)
    parts = call(
        prepare_kernel,
        (),
        (tokens,),
        [chunk] * CHUNKS,
        [pltpu.SemaphoreType.DMA((nlb * lon,))],
        unread=1,
        room=4,
    )
    f = [permute(part, across) for part in parts]
    bands = call(
        band_kernel, (half_width,), (*parts, beside), jax.ShapeDtypeStruct((2 * rows, width), BF16), [], room=4
    )
    bands = permute(bands, outward)
    g0 = permute(f[0], onward)
    held, *_ = lax.optimization_barrier((parts[0], f[0]))
    qc, keys, vals, wvt = call(
        own_kernel,
        (),
        (held, *parts[1:], beside, projection),
        [
            jax.ShapeDtypeStruct(tile, BF16),
            jax.ShapeDtypeStruct((nlb, groups, 2 * rows, WIDE), BF16),
            jax.ShapeDtypeStruct((nlb, groups, WIDE, 2 * rows), BF16),
            jax.ShapeDtypeStruct((width, width), BF16),
        ],
        [pltpu.VMEM((nlb * rows, width), BF16), pltpu.VMEM((2 * nlb * rows, width), BF16)],
    )
    g1 = permute(after(f[1], qc), onward)
    m, l, acc = call(
        near_kernel,
        (neighbours,),
        (after(qc, f[1], bands), keys, vals),
        carried_shapes,
        [],
        cost=NEAR_COST,
        room=12,
    )
    g2 = permute(after(f[2], m), onward)
    m, l, acc = call(
        across_kernel,
        (neighbours, half_width),
        (*f, bands, projection, wvt, qc, m, l, acc),
        carried_shapes,
        [pltpu.VMEM(((nlb + 2) * rows, width), BF16), key_scratch, val_scratch, *wide_scratch],
        cost=ACROSS_COST,
    )
    early = nlb // CHUNKS * (CHUNKS - 1)
    early_keys, early_vals = call(
        early_kernel,
        (),
        (after(g0, m), g1, projection, wvt),
        [
            jax.ShapeDtypeStruct((early, groups, rows, WIDE), BF16),
            jax.ShapeDtypeStruct((2, early, groups, WIDE, 2 * rows), BF16),
        ],
        [pltpu.VMEM((early * rows, width), BF16)],
        cost=EARLY_COST,
        room=16,
    )
    e = call(
        payload_kernel,
        (half_width,),
        (*f, g0, g1, g2, after(bands, early_keys)),
        jax.ShapeDtypeStruct(((nlb + 2) * rows, width), BF16),
        [],
        room=6,
    )
    e = permute(e, sibling)
    m, l, acc = call(
        onward_kernel,
        (neighbours, half_width),
        (g2, projection, wvt, qc, early_keys, early_vals, m, l, acc),
        carried_shapes,
        [
            key_scratch,
            val_scratch,
        ],
    )
    return call(
        last_kernel,
        (neighbours, half_width),
        (e, projection, wvt, out_weight, qc, m, l, acc),
        jax.ShapeDtypeStruct(tokens.shape, BF16),
        [
            key_scratch,
            val_scratch,
            *wide_scratch,
            pltpu.VMEM((nlb * rows, width), BF16),
        ],
    )


def solution(mesh):
    return jax.shard_map(
        per_device,
        mesh=mesh,
        in_specs=(P(("groups", "lon"), None, None), P(), P(), P(), P()),
        out_specs=P(("groups", "lon"), None, None),
        check_vma=False,
    )
```

```python
import math

import jax
import jax.numpy as jnp
from jax import lax
from jax.experimental import pallas as pl
from jax.experimental.pallas import tpu as pltpu
from jax.sharding import PartitionSpec as P

HEADS = 16
HEAD = 64
PACK = 4
WIDE = PACK * HEAD
CHUNKS = 3
NEVER = -1e37
BF16 = jnp.bfloat16
F32 = jnp.float32
SCALE = math.log2(math.e) / math.sqrt(HEAD)
MIB = 1024 * 1024
COST = 2000000000
EARLY_COST = 2000000000
NEAR_COST = 2000000000
ACROSS_COST = 2000000000


def lane_head(shape):
    return lax.broadcasted_iota(jnp.int32, shape, len(shape) - 1) // HEAD


def spread(packed):
    lane = lane_head((1, WIDE))
    return jnp.concatenate(
        [packed * (lane == h).astype(F32).astype(BF16) for h in range(PACK)], axis=0
    )


def gather_diagonal(full):
    lane = lane_head((HEAD, WIDE))
    total = full[:HEAD]
    for h in range(1, PACK):
        total = jnp.where(lane == h, full[h * HEAD : (h + 1) * HEAD], total)
    return total


def dot(a, b):
    return jnp.dot(a, b, preferred_element_type=F32)


def dot_nt(a, b):
    return lax.dot_general(a, b, (((1,), (1,)), ((), ())), preferred_element_type=F32)


def update(scores, values_t, carried):
    row_max, total, summed = carried
    new_max = jnp.maximum(row_max, jnp.max(scores, axis=0, keepdims=True))
    exponent = jnp.exp2((scores - new_max) * SCALE)
    factor = jnp.exp2((row_max - new_max) * SCALE)
    total = total * factor + jnp.sum(exponent, axis=0, keepdims=True)
    summed = summed * factor + gather_diagonal(dot(values_t, exponent.astype(BF16)))
    return new_max, total, summed


def halves(pair):
    lane = lax.broadcasted_iota(jnp.int32, pair.shape, 1)
    turned = pltpu.roll(pair, HEAD, 1)
    low = lane < HEAD
    zero = jnp.zeros_like(pair)
    first = (jnp.where(low, pair, zero), jnp.where(low, zero, turned))
    second = (jnp.where(low, turned, zero), jnp.where(low, zero, pair))
    return first, second


def widest_of(hw):
    best, where = hw[0], 0
    for c in range(1, hw.shape[0]):
        larger = hw[c] > best
        best = jnp.where(larger, hw[c], best)
        where = jnp.where(larger, c, where)
    return where


def project_values(wvt, tokens, g, blocks, rows):
    v = dot_nt(wvt[g * WIDE : (g + 1) * WIDE, :], tokens)
    parts = []
    for c in range(0, blocks, 2):
        for left, right in halves(v[:, c * rows : (c + 2) * rows]):
            parts.append((left.astype(BF16), right.astype(BF16)))
    return parts, v[:, blocks * rows :].astype(BF16)


def prepare_kernel(x, f0, f1, f2, sems):
    lon, lat, _ = x.shape
    span = lat * lon // sems.shape[0]
    out = (f0, f1, f2)
    count = f0.shape[0] // span // lon
    copies = []
    for j in range(CHUNKS):
        for c in range(count):
            for o in range(lon):
                at = (c * lon + o) * span
                copies.append(
                    pltpu.make_async_copy(
                        x.at[o, pl.ds((j * count + c) * span, span), :],
                        out[j].at[pl.ds(at, span), :],
                        sems.at[len(copies)],
                    )
                )
                copies[-1].start()
    for copy in copies:
        copy.wait()


def band_kernel(hw, x0, x1, x2, s, bands):
    wide = widest_of(hw)
    lon = s.shape[0]
    rows = bands.shape[0] // 2
    span = rows // lon
    per = x0.shape[0] // rows
    for c in range(CHUNKS * per):

        @pl.when(wide == c)
        def _(c=c):
            at = (c % per) * rows
            bands[:rows, :] = (x0, x1, x2)[c // per][at : at + rows, :]
            for o in range(lon):
                bands[rows + o * span : rows + (o + 1) * span, :] = s[o, c * span : (c + 1) * span, :]


def query_kernel(x0, x1, x2, w, qc, wvt, own, wq, wv, turned, sems):
    width = wq.shape[0]
    groups = width // WIDE
    blocks = qc.shape[0] // groups
    rows = own.shape[0] // blocks
    fetch_v = pltpu.make_async_copy(w.at[:, pl.ds(2 * width, width)], wv, sems.at[0])
    fetch_q = pltpu.make_async_copy(w.at[:, pl.ds(0, width)], wq, sems.at[1])
    fetch_v.start()
    fetch_q.start()
    at = 0
    for part in (x0, x1, x2):
        own[at : at + part.shape[0], :] = part[...]
        at += part.shape[0]
    tiles = [slice(g * WIDE, (g + 1) * WIDE) for g in range(groups)]
    fetch_v.wait()
    for columns in tiles:
        turned[columns, :] = wv[:, columns].T
    put_back = pltpu.make_async_copy(turned, wvt, sems.at[2])
    put_back.start()
    fetch_q.wait()
    for g, columns in enumerate(tiles):
        q = dot(own[...], wq[:, columns]).astype(BF16).astype(F32)
        for b in range(blocks):
            qt = q[b * rows : (b + 1) * rows, :].T
            qc[b * groups + g] = jnp.concatenate(
                [qt[h * HEAD : (h + 1) * HEAD, :] for h in range(PACK)], axis=1
            ).astype(BF16)
    put_back.wait()


def own_kernel(x0, x1, x2, s, w, far_wvt, keys, vals, wk, wvt, both, sems):
    lon, _, width = s.shape
    nlb, groups, rows, _ = keys.shape
    rows //= 2
    span = rows // lon
    fetch_k = pltpu.make_async_copy(w.at[:, pl.ds(width, width)], wk, sems.at[0])
    fetch_v = pltpu.make_async_copy(far_wvt, wvt, sems.at[1])
    fetch_k.start()
    at = 0
    for part in (x0, x1, x2):
        for c in range(part.shape[0] // rows):
            both[2 * at : 2 * at + rows, :] = part[c * rows : (c + 1) * rows, :]
            at += rows
    for c in range(nlb):
        for o in range(lon):
            at = (2 * c + 1) * rows + o * span
            both[at : at + span, :] = s[o, c * span : (c + 1) * span, :]
    tiles = [slice(g * WIDE, (g + 1) * WIDE) for g in range(groups)]
    fetch_k.wait()
    fetch_v.start()
    for g, columns in enumerate(tiles):
        k = dot(both[...], wk[:, columns]).astype(BF16)
        for c in range(nlb):
            keys[c, g] = k[2 * c * rows : 2 * (c + 1) * rows, :]
    fetch_v.wait()
    for g, columns in enumerate(tiles):
        v = dot_nt(wvt[columns, :], both[...]).astype(BF16)
        for c in range(nlb):
            vals[c, g] = v[:, 2 * c * rows : 2 * (c + 1) * rows]


def near_kernel(nbr, qc, keys, vals, m, l, acc):
    nlb, groups, _, _ = keys.shape
    for b in range(nlb):
        c0, c1 = nbr[b, 0], nbr[b, 1]
        for g in range(groups):
            t = b * groups + g
            k = jnp.concatenate([keys[c0, g], keys[c1, g]], axis=0)
            v = jnp.concatenate([vals[c0, g], vals[c1, g]], axis=1)
            scores = dot(k, spread(qc[t]))
            row_max = jnp.max(scores, axis=0, keepdims=True)
            exponent = jnp.exp2((scores - row_max) * SCALE)
            m[t] = row_max
            l[t] = jnp.sum(exponent, axis=0, keepdims=True)
            acc[t] = gather_diagonal(dot(v, exponent.astype(BF16)))


def project_far(tokens, w, wvt, keys, vals, wkeys, wvals):
    nlb, groups, rows, _ = keys.shape
    ks = [
        dot(tokens[...], w[:, g * WIDE : (g + 1) * WIDE]).astype(BF16)
        for g in range(groups)
    ]
    for g in range(groups):
        k = ks[g]
        parts, rest = project_values(wvt, tokens[...], g, nlb, rows)
        for c in range(nlb):
            keys[c, g] = k[c * rows : (c + 1) * rows, :]
            vals[0, c, g] = parts[c][0]
            vals[1, c, g] = parts[c][1]
        if wkeys is not None:
            wkeys[g] = k[nlb * rows :, :]
            wvals[g] = rest


def attend_far(nbr, seen, wide, qc, keys, vals, wkeys, wvals, before, finish):
    nlb = nbr.shape[0]
    groups = qc.shape[0] // nlb
    for b in range(nlb):
        c0, c1 = nbr[b, 0], nbr[b, 1]
        for g in range(groups):
            t = b * groups + g
            q = spread(qc[t])
            ks = [keys[c0, g], keys[c1, g]]
            rows = ks[0].shape[0]
            v = vals[0, c0, g] + vals[1, c1, g]
            if wkeys is None:
                ks = ks + ks
            if wkeys is not None:
                ks.append(wkeys[g])
                v = jnp.concatenate([v, wvals[g]], axis=1)
            scores = dot(jnp.concatenate(ks, axis=0), q)
            pieces = [scores[:rows], scores[rows : 2 * rows]]
            if seen is not None:
                pieces[0] += jnp.where(seen[c0] >= 2, 0.0, NEVER)
                pieces[1] += jnp.where(seen[c1] >= 2, 0.0, NEVER)
            if wkeys is not None:
                member = (c0 == wide) | (c1 == wide)
                pieces.append(scores[2 * rows :] + jnp.where(member, 0.0, NEVER))
            scores = jnp.concatenate(pieces, axis=0)
            finish(b, g, *update(scores, v, tuple(r[t] for r in before)))


def keep(m, l, acc, groups):
    def store(b, g, row_max, total, summed):
        t = b * groups + g
        m[t], l[t], acc[t] = row_max, total, summed

    return store


def across_kernel(nbr, hw, f0, f1, f2, bands, w, wvt, qc, m_in, l_in, acc_in,
                  m, l, acc, tokens, keys, vals, wkeys, wvals):
    at = 0
    for part in (f0, f1, f2, bands):
        tokens[at : at + part.shape[0], :] = part[...]
        at += part.shape[0]
    project_far(tokens, w, wvt, keys, vals, wkeys, wvals)
    attend_far(nbr, hw, widest_of(hw), qc, keys, vals, wkeys, wvals, (m_in, l_in, acc_in), keep(m, l, acc, keys.shape[1]))


def early_kernel(g0, g1, w, wvt, keys, vals, tokens):
    tokens[: g0.shape[0], :] = g0[...]
    tokens[g0.shape[0] :, :] = g1[...]
    project_far(tokens, w, wvt, keys, vals, None, None)


def onward_kernel(nbr, hw, g2, w, wvt, qc, early_keys, early_vals, m_in, l_in, acc_in, m, l, acc, keys, vals):
    early = early_keys.shape[0]
    keys[:early] = early_keys[...]
    vals[:, :early] = early_vals[...]
    project_far(g2, w, wvt, keys.at[early:], vals.at[:, early:], None, None)
    store = keep(m, l, acc, keys.shape[1])
    attend_far(nbr, hw, None, qc, keys, vals, None, None, (m_in, l_in, acc_in), store)


def payload_kernel(hw, f0, f1, f2, g0, g1, g2, bands, out):
    here = lax.axis_index("lon")
    wide = widest_of(hw)
    size = f0.shape[0]
    rows = bands.shape[0] // 2
    per = size // rows
    base = CHUNKS * size

    def fill(sent, other):
        for j in range(CHUNKS):
            out[j * size : (j + 1) * size, :] = sent[j][...]
        out[base : base + rows, :] = bands[rows:, :]
        for c in range(CHUNKS * per):

            @pl.when(wide == c)
            def _(c=c):
                at = (c % per) * rows
                out[base + rows :, :] = other[c // per][at : at + rows, :]

    kind = (here ^ (here >> 1)) & 1

    @pl.when(kind == 0)
    def _():
        fill((f0, f1, f2), (g0, g1, g2))

    @pl.when(kind != 0)
    def _():
        fill((g0, g1, g2), (f0, f1, f2))


def last_kernel(nbr, hw, e, w, wvt, wout, qc, m_in, l_in, acc_in, out, keys, vals, wkeys, wvals, attended):
    nlb, groups, rows, _ = keys.shape
    lon = out.shape[0]
    span = rows // lon

    def store(b, g, _, total, summed):
        done = (summed * (1.0 / total)).T
        attended[b * rows : (b + 1) * rows, g * WIDE : (g + 1) * WIDE] = jnp.concatenate(
            [done[h * HEAD : (h + 1) * HEAD, :] for h in range(PACK)], axis=1
        ).astype(BF16)

    project_far(e, w, wvt, keys, vals, wkeys, wvals)
    attend_far(nbr, None, widest_of(hw), qc, keys, vals, wkeys, wvals, (m_in, l_in, acc_in), store)
    for g in range(groups):
        r = dot(attended[...], wout[:, g * WIDE : (g + 1) * WIDE]).astype(BF16)
        for b in range(nlb):
            for o in range(lon):
                at = b * rows + o * span
                out[o, b * span : (b + 1) * span, g * WIDE : (g + 1) * WIDE] = r[at : at + span, :]


def call(kernel, scalars, arrays, outs, scratch, unread=0, unwritten=0, cost=COST, room=22):
    smem = pl.BlockSpec(memory_space=pltpu.SMEM)
    vmem = pl.BlockSpec(memory_space=pltpu.VMEM)
    single = not isinstance(outs, (list, tuple))
    specs = [vmem] * (len(arrays) - unread) + [pl.BlockSpec(memory_space=pltpu.HBM)] * unread
    read = len(arrays) - unread
    arrays = [
        a if i < read else pltpu.with_memory_space_constraint(a, pltpu.HBM)
        for i, a in enumerate(arrays)
    ]
    return pl.pallas_call(
        kernel,
        out_shape=outs,
        in_specs=[smem] * len(scalars) + specs,
        out_specs=vmem
        if single
        else [vmem] * (len(outs) - unwritten) + [pl.BlockSpec(memory_space=pltpu.HBM)] * unwritten,
        scratch_shapes=scratch,
        compiler_params=pltpu.CompilerParams(vmem_limit_bytes=room * MIB),
        cost_estimate=pl.CostEstimate(flops=cost, bytes_accessed=1000, transcendentals=0),
    )(*scalars, *arrays)


def after(value, *others):
    return lax.optimization_barrier((value, *others))[0]


def per_device(tokens, projection, out_weight, half_width, neighbours):
    lon, lat, width = tokens.shape
    nlb = neighbours.shape[0]
    span = lat // nlb
    rows = lon * span
    groups = width // WIDE
    tiles = nlb * groups
    count = lax.axis_size("lon")
    devices = range(count)

    def permute(block, step):
        return lax.ppermute(block, "lon", [(i, step(i) % count) for i in devices])

    def sibling(i):
        return i ^ 1

    def across(i):
        return i ^ 2

    def onward(i):
        return i - 4 if i & 2 else i + 4

    def outward(i):
        return i - 4 if i & 1 else i + 4

    tile = (tiles, HEAD, WIDE)
    row = (tiles, 1, WIDE)
    carried_shapes = [
        jax.ShapeDtypeStruct(row, F32),
        jax.ShapeDtypeStruct(row, F32),
        jax.ShapeDtypeStruct(tile, F32),
    ]
    key_scratch = pltpu.VMEM((nlb, groups, rows, WIDE), BF16)
    val_scratch = pltpu.VMEM((2, nlb, groups, WIDE, 2 * rows), BF16)
    wide_scratch = [
        pltpu.VMEM((groups, 2 * rows, WIDE), BF16),
        pltpu.VMEM((groups, WIDE, 2 * rows), BF16),
    ]

    beside = permute(tokens, sibling)
    chunk = jax.ShapeDtypeStruct((nlb * rows // CHUNKS, width), BF16)
    parts = call(
        prepare_kernel,
        (),
        (tokens,),
        [chunk] * CHUNKS,
        [pltpu.SemaphoreType.DMA((nlb * lon,))],
        unread=1,
        room=4,
    )
    f = [permute(parts[0], across)]
    weight = jax.ShapeDtypeStruct((width, width), BF16)
    qc, far_wvt = call(
        query_kernel,
        (),
        (*parts, projection),
        [jax.ShapeDtypeStruct(tile, BF16), pltpu.HBM(weight.shape, BF16)],
        [
            pltpu.VMEM((nlb * rows, width), BF16),
            pltpu.VMEM((width, width), BF16),
            pltpu.VMEM((width, width), BF16),
            pltpu.VMEM((width, width), BF16),
            pltpu.SemaphoreType.DMA((3,)),
        ],
        unread=1,
        unwritten=1,
        room=16,
    )
    bands = call(
        band_kernel,
        (half_width,),
        (*parts, after(beside, qc)),
        jax.ShapeDtypeStruct((2 * rows, width), BF16),
        [],
        room=4,
    )
    f.append(permute(after(parts[1], qc), across))
    f.append(permute(after(parts[2], bands), across))
    bands = permute(bands, outward)
    g0 = permute(f[0], onward)
    held, *_ = lax.optimization_barrier((parts[0], f[0]))
    keys, vals, wk, wvt = call(
        own_kernel,
        (),
        (held, *parts[1:], beside, projection, far_wvt),
        [
            jax.ShapeDtypeStruct((nlb, groups, 2 * rows, WIDE), BF16),
            jax.ShapeDtypeStruct((nlb, groups, WIDE, 2 * rows), BF16),
            weight,
            weight,
        ],
        [pltpu.VMEM((2 * nlb * rows, width), BF16), pltpu.SemaphoreType.DMA((2,))],
        unread=2,
    )
    g1 = permute(after(f[1], keys), onward)
    m, l, acc = call(
        near_kernel,
        (neighbours,),
        (after(qc, f[1], bands), keys, vals),
        carried_shapes,
        [],
        cost=NEAR_COST,
        room=12,
    )
    g2 = permute(after(f[2], m), onward)
    m, l, acc = call(
        across_kernel,
        (neighbours, half_width),
        (*f, bands, wk, wvt, qc, m, l, acc),
        carried_shapes,
        [pltpu.VMEM(((nlb + 2) * rows, width), BF16), key_scratch, val_scratch, *wide_scratch],
        cost=ACROSS_COST,
    )
    early = nlb // CHUNKS * (CHUNKS - 1)
    early_keys, early_vals = call(
        early_kernel,
        (),
        (after(g0, m), g1, wk, wvt),
        [
            jax.ShapeDtypeStruct((early, groups, rows, WIDE), BF16),
            jax.ShapeDtypeStruct((2, early, groups, WIDE, 2 * rows), BF16),
        ],
        [pltpu.VMEM((early * rows, width), BF16)],
        cost=EARLY_COST,
        room=16,
    )
    e = call(
        payload_kernel,
        (half_width,),
        (*f, g0, g1, g2, after(bands, early_keys)),
        jax.ShapeDtypeStruct(((nlb + 2) * rows, width), BF16),
        [],
        room=6,
    )
    e = permute(e, sibling)
    m, l, acc = call(
        onward_kernel,
        (neighbours, half_width),
        (g2, wk, wvt, qc, early_keys, early_vals, m, l, acc),
        carried_shapes,
        [
            key_scratch,
            val_scratch,
        ],
    )
    return call(
        last_kernel,
        (neighbours, half_width),
        (e, wk, wvt, out_weight, qc, m, l, acc),
        jax.ShapeDtypeStruct(tokens.shape, BF16),
        [
            key_scratch,
            val_scratch,
            *wide_scratch,
            pltpu.VMEM((nlb * rows, width), BF16),
        ],
    )


def solution(mesh):
    return jax.shard_map(
        per_device,
        mesh=mesh,
        in_specs=(P(("groups", "lon"), None, None), P(), P(), P(), P()),
        out_specs=P(("groups", "lon"), None, None),
        check_vma=False,
    )
```

```python
import math

import jax
import jax.numpy as jnp
from jax import lax
from jax.experimental import pallas as pl
from jax.experimental.pallas import tpu as pltpu
from jax.sharding import PartitionSpec as P

HEADS = 16
HEAD = 64
PACK = 4
WIDE = PACK * HEAD
CHUNKS = 3
NEVER = -1e37
BF16 = jnp.bfloat16
F32 = jnp.float32
SCALE = math.log2(math.e) / math.sqrt(HEAD)
MIB = 1024 * 1024
COST = 2000000000
EARLY_COST = 4000000000
NEAR_COST = 2000000000
ACROSS_COST = 2000000000


def lane_head(shape):
    return lax.broadcasted_iota(jnp.int32, shape, len(shape) - 1) // HEAD


def spread(packed):
    lane = lane_head((1, WIDE))
    return jnp.concatenate(
        [packed * (lane == h).astype(F32).astype(BF16) for h in range(PACK)], axis=0
    )


def gather_diagonal(full):
    lane = lane_head((HEAD, WIDE))
    total = full[:HEAD]
    for h in range(1, PACK):
        total = jnp.where(lane == h, full[h * HEAD : (h + 1) * HEAD], total)
    return total


def dot(a, b):
    return jnp.dot(a, b, preferred_element_type=F32)


def dot_nt(a, b):
    return lax.dot_general(a, b, (((1,), (1,)), ((), ())), preferred_element_type=F32)


def update(scores, values_t, carried):
    row_max, total, summed = carried
    new_max = jnp.maximum(row_max, jnp.max(scores, axis=0, keepdims=True))
    exponent = jnp.exp2((scores - new_max) * SCALE)
    factor = jnp.exp2((row_max - new_max) * SCALE)
    total = total * factor + jnp.sum(exponent, axis=0, keepdims=True)
    summed = summed * factor + gather_diagonal(dot(values_t, exponent.astype(BF16)))
    return new_max, total, summed


def halves(pair):
    lane = lax.broadcasted_iota(jnp.int32, pair.shape, 1)
    turned = pltpu.roll(pair, HEAD, 1)
    low = lane < HEAD
    zero = jnp.zeros_like(pair)
    first = (jnp.where(low, pair, zero), jnp.where(low, zero, turned))
    second = (jnp.where(low, turned, zero), jnp.where(low, zero, pair))
    return first, second


def widest_of(hw):
    best, where = hw[0], 0
    for c in range(1, hw.shape[0]):
        larger = hw[c] > best
        best = jnp.where(larger, hw[c], best)
        where = jnp.where(larger, c, where)
    return where


def project_values(wvt, tokens, g, blocks, rows):
    v = dot_nt(wvt[g * WIDE : (g + 1) * WIDE, :], tokens)
    parts = []
    for c in range(0, blocks, 2):
        for left, right in halves(v[:, c * rows : (c + 2) * rows]):
            parts.append((left.astype(BF16), right.astype(BF16)))
    return parts, v[:, blocks * rows :].astype(BF16)


def prepare_kernel(x, f0, f1, f2, sems):
    lon, lat, _ = x.shape
    span = lat * lon // sems.shape[0]
    out = (f0, f1, f2)
    count = f0.shape[0] // span // lon
    copies = []
    for j in range(CHUNKS):
        for c in range(count):
            for o in range(lon):
                at = (c * lon + o) * span
                copies.append(
                    pltpu.make_async_copy(
                        x.at[o, pl.ds((j * count + c) * span, span), :],
                        out[j].at[pl.ds(at, span), :],
                        sems.at[len(copies)],
                    )
                )
                copies[-1].start()
    for copy in copies:
        copy.wait()


def band_kernel(hw, x0, x1, x2, s, bands):
    wide = widest_of(hw)
    lon = s.shape[0]
    rows = bands.shape[0] // 2
    span = rows // lon
    per = x0.shape[0] // rows
    for c in range(CHUNKS * per):

        @pl.when(wide == c)
        def _(c=c):
            at = (c % per) * rows
            bands[:rows, :] = (x0, x1, x2)[c // per][at : at + rows, :]
            for o in range(lon):
                bands[rows + o * span : rows + (o + 1) * span, :] = s[o, c * span : (c + 1) * span, :]


def own_kernel(x0, x1, x2, s, w, qc, keys, vals, wk, wvt, own, both, wq, wv, sems):
    lon, _, width = s.shape
    nlb, groups, rows, _ = keys.shape
    rows //= 2
    span = rows // lon
    fetch = [
        pltpu.make_async_copy(w.at[:, pl.ds(which * width, width)], place, sems.at[which])
        for which, place in ((0, wq), (1, wk), (2, wv))
    ]
    fetch[1].start()
    at = 0
    for part in (x0, x1, x2):
        for c in range(part.shape[0] // rows):
            block = part[c * rows : (c + 1) * rows, :]
            own[at : at + rows, :] = block
            both[2 * at : 2 * at + rows, :] = block
            at += rows
    for c in range(nlb):
        for o in range(lon):
            at = (2 * c + 1) * rows + o * span
            both[at : at + span, :] = s[o, c * span : (c + 1) * span, :]
    tiles = [slice(g * WIDE, (g + 1) * WIDE) for g in range(groups)]
    fetch[1].wait()
    fetch[0].start()
    fetch[2].start()
    for g, columns in enumerate(tiles):
        k = dot(both[...], wk[:, columns]).astype(BF16)
        for c in range(nlb):
            keys[c, g] = k[2 * c * rows : 2 * (c + 1) * rows, :]
    fetch[0].wait()
    fetch[2].wait()
    for g, columns in enumerate(tiles):
        q = dot(own[...], wq[:, columns]).astype(BF16).astype(F32)
        for b in range(nlb):
            qt = q[b * rows : (b + 1) * rows, :].T
            qc[b * groups + g] = jnp.concatenate(
                [qt[h * HEAD : (h + 1) * HEAD, :] for h in range(PACK)], axis=1
            ).astype(BF16)
        wvt[columns, :] = wv[:, columns].T
        v = dot_nt(wvt[columns, :], both[...]).astype(BF16)
        for c in range(nlb):
            vals[c, g] = v[:, 2 * c * rows : 2 * (c + 1) * rows]


def near_kernel(nbr, qc, keys, vals, m, l, acc):
    nlb, groups, _, _ = keys.shape
    for b in range(nlb):
        c0, c1 = nbr[b, 0], nbr[b, 1]
        for g in range(groups):
            t = b * groups + g
            k = jnp.concatenate([keys[c0, g], keys[c1, g]], axis=0)
            v = jnp.concatenate([vals[c0, g], vals[c1, g]], axis=1)
            scores = dot(k, spread(qc[t]))
            row_max = jnp.max(scores, axis=0, keepdims=True)
            exponent = jnp.exp2((scores - row_max) * SCALE)
            m[t] = row_max
            l[t] = jnp.sum(exponent, axis=0, keepdims=True)
            acc[t] = gather_diagonal(dot(v, exponent.astype(BF16)))


def project_far(tokens, w, wvt, keys, vals, wkeys, wvals):
    nlb, groups, rows, _ = keys.shape
    ks = [
        dot(tokens[...], w[:, g * WIDE : (g + 1) * WIDE]).astype(BF16)
        for g in range(groups)
    ]
    for g in range(groups):
        k = ks[g]
        parts, rest = project_values(wvt, tokens[...], g, nlb, rows)
        for c in range(nlb):
            keys[c, g] = k[c * rows : (c + 1) * rows, :]
            vals[0, c, g] = parts[c][0]
            vals[1, c, g] = parts[c][1]
        if wkeys is not None:
            wkeys[g] = k[nlb * rows :, :]
            wvals[g] = rest


def attend_far(nbr, seen, wide, qc, keys, vals, wkeys, wvals, before, finish):
    nlb = nbr.shape[0]
    groups = qc.shape[0] // nlb
    for b in range(nlb):
        c0, c1 = nbr[b, 0], nbr[b, 1]
        for g in range(groups):
            t = b * groups + g
            q = spread(qc[t])
            ks = [keys[c0, g], keys[c1, g]]
            rows = ks[0].shape[0]
            v = vals[0, c0, g] + vals[1, c1, g]
            if wkeys is None:
                ks = ks + ks
            if wkeys is not None:
                ks.append(wkeys[g])
                v = jnp.concatenate([v, wvals[g]], axis=1)
            scores = dot(jnp.concatenate(ks, axis=0), q)
            pieces = [scores[:rows], scores[rows : 2 * rows]]
            if seen is not None:
                pieces[0] += jnp.where(seen[c0] >= 2, 0.0, NEVER)
                pieces[1] += jnp.where(seen[c1] >= 2, 0.0, NEVER)
            if wkeys is not None:
                member = (c0 == wide) | (c1 == wide)
                pieces.append(scores[2 * rows :] + jnp.where(member, 0.0, NEVER))
            scores = jnp.concatenate(pieces, axis=0)
            finish(b, g, *update(scores, v, tuple(r[t] for r in before)))


def keep(m, l, acc, groups):
    def store(b, g, row_max, total, summed):
        t = b * groups + g
        m[t], l[t], acc[t] = row_max, total, summed

    return store


def across_kernel(nbr, hw, f0, f1, f2, bands, w, wvt, qc, m_in, l_in, acc_in,
                  m, l, acc, tokens, keys, vals, wkeys, wvals):
    at = 0
    for part in (f0, f1, f2, bands):
        tokens[at : at + part.shape[0], :] = part[...]
        at += part.shape[0]
    project_far(tokens, w, wvt, keys, vals, wkeys, wvals)
    attend_far(nbr, hw, widest_of(hw), qc, keys, vals, wkeys, wvals, (m_in, l_in, acc_in), keep(m, l, acc, keys.shape[1]))


def early_kernel(g0, g1, w, wvt, keys, vals, tokens):
    tokens[: g0.shape[0], :] = g0[...]
    tokens[g0.shape[0] :, :] = g1[...]
    project_far(tokens, w, wvt, keys, vals, None, None)


def onward_kernel(nbr, hw, g2, w, wvt, qc, early_keys, early_vals, m_in, l_in, acc_in, m, l, acc, keys, vals):
    early = early_keys.shape[0]
    keys[:early] = early_keys[...]
    vals[:, :early] = early_vals[...]
    project_far(g2, w, wvt, keys.at[early:], vals.at[:, early:], None, None)
    store = keep(m, l, acc, keys.shape[1])
    attend_far(nbr, hw, None, qc, keys, vals, None, None, (m_in, l_in, acc_in), store)


def payload_kernel(hw, f0, f1, f2, g0, g1, g2, bands, out):
    here = lax.axis_index("lon")
    wide = widest_of(hw)
    size = f0.shape[0]
    rows = bands.shape[0] // 2
    per = size // rows
    base = CHUNKS * size

    def fill(sent, other):
        for j in range(CHUNKS):
            out[j * size : (j + 1) * size, :] = sent[j][...]
        out[base : base + rows, :] = bands[rows:, :]
        for c in range(CHUNKS * per):

            @pl.when(wide == c)
            def _(c=c):
                at = (c % per) * rows
                out[base + rows :, :] = other[c // per][at : at + rows, :]

    kind = (here ^ (here >> 1)) & 1

    @pl.when(kind == 0)
    def _():
        fill((f0, f1, f2), (g0, g1, g2))

    @pl.when(kind != 0)
    def _():
        fill((g0, g1, g2), (f0, f1, f2))


def last_kernel(nbr, hw, e, w, wvt, wout, qc, m_in, l_in, acc_in, out, keys, vals, wkeys, wvals, attended):
    nlb, groups, rows, _ = keys.shape
    lon = out.shape[0]
    span = rows // lon

    def store(b, g, _, total, summed):
        done = (summed * (1.0 / total)).T
        attended[b * rows : (b + 1) * rows, g * WIDE : (g + 1) * WIDE] = jnp.concatenate(
            [done[h * HEAD : (h + 1) * HEAD, :] for h in range(PACK)], axis=1
        ).astype(BF16)

    project_far(e, w, wvt, keys, vals, wkeys, wvals)
    attend_far(nbr, None, widest_of(hw), qc, keys, vals, wkeys, wvals, (m_in, l_in, acc_in), store)
    for g in range(groups):
        r = dot(attended[...], wout[:, g * WIDE : (g + 1) * WIDE]).astype(BF16)
        for b in range(nlb):
            for o in range(lon):
                at = b * rows + o * span
                out[o, b * span : (b + 1) * span, g * WIDE : (g + 1) * WIDE] = r[at : at + span, :]


def call(kernel, scalars, arrays, outs, scratch, unread=0, cost=COST, room=22):
    smem = pl.BlockSpec(memory_space=pltpu.SMEM)
    vmem = pl.BlockSpec(memory_space=pltpu.VMEM)
    single = not isinstance(outs, (list, tuple))
    specs = [vmem] * (len(arrays) - unread) + [pl.BlockSpec(memory_space=pltpu.HBM)] * unread
    read = len(arrays) - unread
    arrays = [
        a if i < read else pltpu.with_memory_space_constraint(a, pltpu.HBM)
        for i, a in enumerate(arrays)
    ]
    return pl.pallas_call(
        kernel,
        out_shape=outs,
        in_specs=[smem] * len(scalars) + specs,
        out_specs=vmem if single else [vmem] * len(outs),
        scratch_shapes=scratch,
        compiler_params=pltpu.CompilerParams(vmem_limit_bytes=room * MIB),
        cost_estimate=pl.CostEstimate(flops=cost, bytes_accessed=1000, transcendentals=0),
    )(*scalars, *arrays)


def after(value, *others):
    return lax.optimization_barrier((value, *others))[0]


def per_device(tokens, projection, out_weight, half_width, neighbours):
    lon, lat, width = tokens.shape
    nlb = neighbours.shape[0]
    span = lat // nlb
    rows = lon * span
    groups = width // WIDE
    tiles = nlb * groups
    count = lax.axis_size("lon")
    devices = range(count)

    def permute(block, step):
        return lax.ppermute(block, "lon", [(i, step(i) % count) for i in devices])

    def sibling(i):
        return i ^ 1

    def across(i):
        return i ^ 2

    def onward(i):
        return i - 4 if i & 2 else i + 4

    def outward(i):
        return i - 4 if i & 1 else i + 4

    tile = (tiles, HEAD, WIDE)
    row = (tiles, 1, WIDE)
    carried_shapes = [
        jax.ShapeDtypeStruct(row, F32),
        jax.ShapeDtypeStruct(row, F32),
        jax.ShapeDtypeStruct(tile, F32),
    ]
    key_scratch = pltpu.VMEM((nlb, groups, rows, WIDE), BF16)
    val_scratch = pltpu.VMEM((2, nlb, groups, WIDE, 2 * rows), BF16)
    wide_scratch = [
        pltpu.VMEM((groups, 2 * rows, WIDE), BF16),
        pltpu.VMEM((groups, WIDE, 2 * rows), BF16),
    ]

    beside = permute(tokens, sibling)
    chunk = jax.ShapeDtypeStruct((nlb * rows // CHUNKS, width), BF16)
    parts = call(
        prepare_kernel,
        (),
        (tokens,),
        [chunk] * CHUNKS,
        [pltpu.SemaphoreType.DMA((nlb * lon,))],
        unread=1,
        room=4,
    )
    f = [permute(part, across) for part in parts]
    bands = call(
        band_kernel, (half_width,), (*parts, beside), jax.ShapeDtypeStruct((2 * rows, width), BF16), [], room=4
    )
    bands = permute(bands, outward)
    g0 = permute(f[0], onward)
    held, *_ = lax.optimization_barrier((parts[0], f[0]))
    qc, keys, vals, wk, wvt = call(
        own_kernel,
        (),
        (held, *parts[1:], beside, projection),
        [
            jax.ShapeDtypeStruct(tile, BF16),
            jax.ShapeDtypeStruct((nlb, groups, 2 * rows, WIDE), BF16),
            jax.ShapeDtypeStruct((nlb, groups, WIDE, 2 * rows), BF16),
            jax.ShapeDtypeStruct((width, width), BF16),
            jax.ShapeDtypeStruct((width, width), BF16),
        ],
        [
            pltpu.VMEM((nlb * rows, width), BF16),
            pltpu.VMEM((2 * nlb * rows, width), BF16),
            pltpu.VMEM((width, width), BF16),
            pltpu.VMEM((width, width), BF16),
            pltpu.SemaphoreType.DMA((3,)),
        ],
        unread=1,
    )
    g1 = permute(after(f[1], qc), onward)
    m, l, acc = call(
        near_kernel,
        (neighbours,),
        (after(qc, f[1], bands), keys, vals),
        carried_shapes,
        [],
        cost=NEAR_COST,
        room=12,
    )
    g2 = permute(after(f[2], m), onward)
    m, l, acc = call(
        across_kernel,
        (neighbours, half_width),
        (*f, bands, wk, wvt, qc, m, l, acc),
        carried_shapes,
        [pltpu.VMEM(((nlb + 2) * rows, width), BF16), key_scratch, val_scratch, *wide_scratch],
        cost=ACROSS_COST,
    )
    early = nlb // CHUNKS * (CHUNKS - 1)
    early_keys, early_vals = call(
        early_kernel,
        (),
        (after(g0, m), g1, wk, wvt),
        [
            jax.ShapeDtypeStruct((early, groups, rows, WIDE), BF16),
            jax.ShapeDtypeStruct((2, early, groups, WIDE, 2 * rows), BF16),
        ],
        [pltpu.VMEM((early * rows, width), BF16)],
        cost=EARLY_COST,
        room=16,
    )
    e = call(
        payload_kernel,
        (half_width,),
        (*f, g0, g1, g2, after(bands, early_keys)),
        jax.ShapeDtypeStruct(((nlb + 2) * rows, width), BF16),
        [],
        room=6,
    )
    e = permute(e, sibling)
    m, l, acc = call(
        onward_kernel,
        (neighbours, half_width),
        (g2, wk, wvt, qc, early_keys, early_vals, m, l, acc),
        carried_shapes,
        [
            key_scratch,
            val_scratch,
        ],
    )
    return call(
        last_kernel,
        (neighbours, half_width),
        (e, wk, wvt, out_weight, qc, m, l, acc),
        jax.ShapeDtypeStruct(tokens.shape, BF16),
        [
            key_scratch,
            val_scratch,
            *wide_scratch,
            pltpu.VMEM((nlb * rows, width), BF16),
        ],
    )


def solution(mesh):
    return jax.shard_map(
        per_device,
        mesh=mesh,
        in_specs=(P(("groups", "lon"), None, None), P(), P(), P(), P()),
        out_specs=P(("groups", "lon"), None, None),
        check_vma=False,
    )
```

```python
import math

import jax
import jax.numpy as jnp
from jax import lax
from jax.experimental import pallas as pl
from jax.experimental.pallas import tpu as pltpu
from jax.sharding import PartitionSpec as P

HEADS = 16
HEAD = 64
PACK = 4
WIDE = PACK * HEAD
CHUNKS = 3
NEVER = -1e37
BF16 = jnp.bfloat16
F32 = jnp.float32
SCALE = math.log2(math.e) / math.sqrt(HEAD)
MIB = 1024 * 1024
COST = 2000000000
EARLY_COST = 4000000000
NEAR_COST = 2000000000
ACROSS_COST = 2000000000


def lane_head(shape):
    return lax.broadcasted_iota(jnp.int32, shape, len(shape) - 1) // HEAD


def spread(packed):
    lane = lane_head((1, WIDE))
    return jnp.concatenate(
        [packed * (lane == h).astype(F32).astype(BF16) for h in range(PACK)], axis=0
    )


def gather_diagonal(full):
    lane = lane_head((HEAD, WIDE))
    total = full[:HEAD]
    for h in range(1, PACK):
        total = jnp.where(lane == h, full[h * HEAD : (h + 1) * HEAD], total)
    return total


def dot(a, b):
    return jnp.dot(a, b, preferred_element_type=F32)


def dot_nt(a, b):
    return lax.dot_general(a, b, (((1,), (1,)), ((), ())), preferred_element_type=F32)


def update(scores, values_t, carried):
    row_max, total, summed = carried
    new_max = jnp.maximum(row_max, jnp.max(scores, axis=0, keepdims=True))
    exponent = jnp.exp2((scores - new_max) * SCALE)
    factor = jnp.exp2((row_max - new_max) * SCALE)
    total = total * factor + jnp.sum(exponent, axis=0, keepdims=True)
    summed = summed * factor + gather_diagonal(dot(values_t, exponent.astype(BF16)))
    return new_max, total, summed


def halves(pair):
    lane = lax.broadcasted_iota(jnp.int32, pair.shape, 1)
    turned = pltpu.roll(pair, HEAD, 1)
    low = lane < HEAD
    zero = jnp.zeros_like(pair)
    first = (jnp.where(low, pair, zero), jnp.where(low, zero, turned))
    second = (jnp.where(low, turned, zero), jnp.where(low, zero, pair))
    return first, second


def widest_of(hw):
    best, where = hw[0], 0
    for c in range(1, hw.shape[0]):
        larger = hw[c] > best
        best = jnp.where(larger, hw[c], best)
        where = jnp.where(larger, c, where)
    return where


def project_values(wvt, tokens, g, blocks, rows):
    v = dot_nt(wvt[g * WIDE : (g + 1) * WIDE, :], tokens)
    parts = []
    for c in range(0, blocks, 2):
        for left, right in halves(v[:, c * rows : (c + 2) * rows]):
            parts.append((left.astype(BF16), right.astype(BF16)))
    return parts, v[:, blocks * rows :].astype(BF16)


def prepare_kernel(x, f0, f1, f2, sems):
    lon, lat, _ = x.shape
    span = lat * lon // sems.shape[0]
    out = (f0, f1, f2)
    count = f0.shape[0] // span // lon
    copies = []
    for j in range(CHUNKS):
        for c in range(count):
            for o in range(lon):
                at = (c * lon + o) * span
                copies.append(
                    pltpu.make_async_copy(
                        x.at[o, pl.ds((j * count + c) * span, span), :],
                        out[j].at[pl.ds(at, span), :],
                        sems.at[len(copies)],
                    )
                )
                copies[-1].start()
    for copy in copies:
        copy.wait()


def band_kernel(hw, x0, x1, x2, s, bands):
    wide = widest_of(hw)
    lon = s.shape[0]
    rows = bands.shape[0] // 2
    span = rows // lon
    per = x0.shape[0] // rows
    for c in range(CHUNKS * per):

        @pl.when(wide == c)
        def _(c=c):
            at = (c % per) * rows
            bands[:rows, :] = (x0, x1, x2)[c // per][at : at + rows, :]
            for o in range(lon):
                bands[rows + o * span : rows + (o + 1) * span, :] = s[o, c * span : (c + 1) * span, :]


def own_kernel(x0, x1, x2, s, w, qc, keys, vals, wk, wvt, own, both, wq, wv, sems):
    lon, _, width = s.shape
    nlb, groups, rows, _ = keys.shape
    rows //= 2
    span = rows // lon
    fetch = [
        pltpu.make_async_copy(w.at[:, pl.ds(which * width, width)], place, sems.at[which])
        for which, place in ((0, wq), (1, wk), (2, wv))
    ]
    fetch[1].start()
    at = 0
    for part in (x0, x1, x2):
        for c in range(part.shape[0] // rows):
            block = part[c * rows : (c + 1) * rows, :]
            own[at : at + rows, :] = block
            both[2 * at : 2 * at + rows, :] = block
            at += rows
    for c in range(nlb):
        for o in range(lon):
            at = (2 * c + 1) * rows + o * span
            both[at : at + span, :] = s[o, c * span : (c + 1) * span, :]
    tiles = [slice(g * WIDE, (g + 1) * WIDE) for g in range(groups)]
    fetch[1].wait()
    fetch[2].start()
    fetch[0].start()
    for g, columns in enumerate(tiles):
        if g == groups // 2:
            fetch[2].wait()
        if g >= groups // 2:
            for turned in tiles[2 * (g - groups // 2) : 2 * (g - groups // 2) + 2]:
                wvt[turned, :] = wv[:, turned].T
        k = dot(both[...], wk[:, columns]).astype(BF16)
        for c in range(nlb):
            keys[c, g] = k[2 * c * rows : 2 * (c + 1) * rows, :]
    fetch[0].wait()
    for g, columns in enumerate(tiles):
        q = dot(own[...], wq[:, columns]).astype(BF16).astype(F32)
        for b in range(nlb):
            qt = q[b * rows : (b + 1) * rows, :].T
            qc[b * groups + g] = jnp.concatenate(
                [qt[h * HEAD : (h + 1) * HEAD, :] for h in range(PACK)], axis=1
            ).astype(BF16)
        v = dot_nt(wvt[columns, :], both[...]).astype(BF16)
        for c in range(nlb):
            vals[c, g] = v[:, 2 * c * rows : 2 * (c + 1) * rows]


def near_kernel(nbr, qc, keys, vals, m, l, acc):
    nlb, groups, _, _ = keys.shape
    for b in range(nlb):
        c0, c1 = nbr[b, 0], nbr[b, 1]
        for g in range(groups):
            t = b * groups + g
            k = jnp.concatenate([keys[c0, g], keys[c1, g]], axis=0)
            v = jnp.concatenate([vals[c0, g], vals[c1, g]], axis=1)
            scores = dot(k, spread(qc[t]))
            row_max = jnp.max(scores, axis=0, keepdims=True)
            exponent = jnp.exp2((scores - row_max) * SCALE)
            m[t] = row_max
            l[t] = jnp.sum(exponent, axis=0, keepdims=True)
            acc[t] = gather_diagonal(dot(v, exponent.astype(BF16)))


def project_far(tokens, w, wvt, keys, vals, wkeys, wvals):
    nlb, groups, rows, _ = keys.shape
    ks = [
        dot(tokens[...], w[:, g * WIDE : (g + 1) * WIDE]).astype(BF16)
        for g in range(groups)
    ]
    for g in range(groups):
        k = ks[g]
        parts, rest = project_values(wvt, tokens[...], g, nlb, rows)
        for c in range(nlb):
            keys[c, g] = k[c * rows : (c + 1) * rows, :]
            vals[0, c, g] = parts[c][0]
            vals[1, c, g] = parts[c][1]
        if wkeys is not None:
            wkeys[g] = k[nlb * rows :, :]
            wvals[g] = rest


def attend_far(nbr, seen, wide, qc, keys, vals, wkeys, wvals, before, finish):
    nlb = nbr.shape[0]
    groups = qc.shape[0] // nlb
    for b in range(nlb):
        c0, c1 = nbr[b, 0], nbr[b, 1]
        for g in range(groups):
            t = b * groups + g
            q = spread(qc[t])
            ks = [keys[c0, g], keys[c1, g]]
            rows = ks[0].shape[0]
            v = vals[0, c0, g] + vals[1, c1, g]
            if wkeys is None:
                ks = ks + ks
            if wkeys is not None:
                ks.append(wkeys[g])
                v = jnp.concatenate([v, wvals[g]], axis=1)
            scores = dot(jnp.concatenate(ks, axis=0), q)
            pieces = [scores[:rows], scores[rows : 2 * rows]]
            if seen is not None:
                pieces[0] += jnp.where(seen[c0] >= 2, 0.0, NEVER)
                pieces[1] += jnp.where(seen[c1] >= 2, 0.0, NEVER)
            if wkeys is not None:
                member = (c0 == wide) | (c1 == wide)
                pieces.append(scores[2 * rows :] + jnp.where(member, 0.0, NEVER))
            scores = jnp.concatenate(pieces, axis=0)
            finish(b, g, *update(scores, v, tuple(r[t] for r in before)))


def keep(m, l, acc, groups):
    def store(b, g, row_max, total, summed):
        t = b * groups + g
        m[t], l[t], acc[t] = row_max, total, summed

    return store


def across_kernel(nbr, hw, f0, f1, f2, bands, w, wvt, qc, m_in, l_in, acc_in,
                  m, l, acc, tokens, keys, vals, wkeys, wvals):
    at = 0
    for part in (f0, f1, f2, bands):
        tokens[at : at + part.shape[0], :] = part[...]
        at += part.shape[0]
    project_far(tokens, w, wvt, keys, vals, wkeys, wvals)
    attend_far(nbr, hw, widest_of(hw), qc, keys, vals, wkeys, wvals, (m_in, l_in, acc_in), keep(m, l, acc, keys.shape[1]))


def early_kernel(g0, g1, w, wvt, keys, vals, tokens):
    tokens[: g0.shape[0], :] = g0[...]
    tokens[g0.shape[0] :, :] = g1[...]
    project_far(tokens, w, wvt, keys, vals, None, None)


def onward_kernel(nbr, hw, g2, w, wvt, qc, early_keys, early_vals, m_in, l_in, acc_in, m, l, acc, keys, vals):
    early = early_keys.shape[0]
    keys[:early] = early_keys[...]
    vals[:, :early] = early_vals[...]
    project_far(g2, w, wvt, keys.at[early:], vals.at[:, early:], None, None)
    store = keep(m, l, acc, keys.shape[1])
    attend_far(nbr, hw, None, qc, keys, vals, None, None, (m_in, l_in, acc_in), store)


def payload_kernel(hw, f0, f1, f2, g0, g1, g2, bands, out):
    here = lax.axis_index("lon")
    wide = widest_of(hw)
    size = f0.shape[0]
    rows = bands.shape[0] // 2
    per = size // rows
    base = CHUNKS * size

    def fill(sent, other):
        for j in range(CHUNKS):
            out[j * size : (j + 1) * size, :] = sent[j][...]
        out[base : base + rows, :] = bands[rows:, :]
        for c in range(CHUNKS * per):

            @pl.when(wide == c)
            def _(c=c):
                at = (c % per) * rows
                out[base + rows :, :] = other[c // per][at : at + rows, :]

    kind = (here ^ (here >> 1)) & 1

    @pl.when(kind == 0)
    def _():
        fill((f0, f1, f2), (g0, g1, g2))

    @pl.when(kind != 0)
    def _():
        fill((g0, g1, g2), (f0, f1, f2))


def last_kernel(nbr, hw, e, w, wvt, wout, qc, m_in, l_in, acc_in, out, keys, vals, wkeys, wvals, attended):
    nlb, groups, rows, _ = keys.shape
    lon = out.shape[0]
    span = rows // lon

    def store(b, g, _, total, summed):
        done = (summed * (1.0 / total)).T
        attended[b * rows : (b + 1) * rows, g * WIDE : (g + 1) * WIDE] = jnp.concatenate(
            [done[h * HEAD : (h + 1) * HEAD, :] for h in range(PACK)], axis=1
        ).astype(BF16)

    project_far(e, w, wvt, keys, vals, wkeys, wvals)
    attend_far(nbr, None, widest_of(hw), qc, keys, vals, wkeys, wvals, (m_in, l_in, acc_in), store)
    for g in range(groups):
        r = dot(attended[...], wout[:, g * WIDE : (g + 1) * WIDE]).astype(BF16)
        for b in range(nlb):
            for o in range(lon):
                at = b * rows + o * span
                out[o, b * span : (b + 1) * span, g * WIDE : (g + 1) * WIDE] = r[at : at + span, :]


def call(kernel, scalars, arrays, outs, scratch, unread=0, cost=COST, room=22):
    smem = pl.BlockSpec(memory_space=pltpu.SMEM)
    vmem = pl.BlockSpec(memory_space=pltpu.VMEM)
    single = not isinstance(outs, (list, tuple))
    specs = [vmem] * (len(arrays) - unread) + [pl.BlockSpec(memory_space=pltpu.HBM)] * unread
    read = len(arrays) - unread
    arrays = [
        a if i < read else pltpu.with_memory_space_constraint(a, pltpu.HBM)
        for i, a in enumerate(arrays)
    ]
    return pl.pallas_call(
        kernel,
        out_shape=outs,
        in_specs=[smem] * len(scalars) + specs,
        out_specs=vmem if single else [vmem] * len(outs),
        scratch_shapes=scratch,
        compiler_params=pltpu.CompilerParams(vmem_limit_bytes=room * MIB),
        cost_estimate=pl.CostEstimate(flops=cost, bytes_accessed=1000, transcendentals=0),
    )(*scalars, *arrays)


def after(value, *others):
    return lax.optimization_barrier((value, *others))[0]


def per_device(tokens, projection, out_weight, half_width, neighbours):
    lon, lat, width = tokens.shape
    nlb = neighbours.shape[0]
    span = lat // nlb
    rows = lon * span
    groups = width // WIDE
    tiles = nlb * groups
    count = lax.axis_size("lon")
    devices = range(count)

    def permute(block, step):
        return lax.ppermute(block, "lon", [(i, step(i) % count) for i in devices])

    def sibling(i):
        return i ^ 1

    def across(i):
        return i ^ 2

    def onward(i):
        return i - 4 if i & 2 else i + 4

    def outward(i):
        return i - 4 if i & 1 else i + 4

    tile = (tiles, HEAD, WIDE)
    row = (tiles, 1, WIDE)
    carried_shapes = [
        jax.ShapeDtypeStruct(row, F32),
        jax.ShapeDtypeStruct(row, F32),
        jax.ShapeDtypeStruct(tile, F32),
    ]
    key_scratch = pltpu.VMEM((nlb, groups, rows, WIDE), BF16)
    val_scratch = pltpu.VMEM((2, nlb, groups, WIDE, 2 * rows), BF16)
    wide_scratch = [
        pltpu.VMEM((groups, 2 * rows, WIDE), BF16),
        pltpu.VMEM((groups, WIDE, 2 * rows), BF16),
    ]

    beside = permute(tokens, sibling)
    chunk = jax.ShapeDtypeStruct((nlb * rows // CHUNKS, width), BF16)
    parts = call(
        prepare_kernel,
        (),
        (tokens,),
        [chunk] * CHUNKS,
        [pltpu.SemaphoreType.DMA((nlb * lon,))],
        unread=1,
        room=4,
    )
    f = [permute(part, across) for part in parts]
    bands = call(
        band_kernel, (half_width,), (*parts, beside), jax.ShapeDtypeStruct((2 * rows, width), BF16), [], room=4
    )
    bands = permute(bands, outward)
    g0 = permute(f[0], onward)
    held, *_ = lax.optimization_barrier((parts[0], f[0]))
    qc, keys, vals, wk, wvt = call(
        own_kernel,
        (),
        (held, *parts[1:], beside, projection),
        [
            jax.ShapeDtypeStruct(tile, BF16),
            jax.ShapeDtypeStruct((nlb, groups, 2 * rows, WIDE), BF16),
            jax.ShapeDtypeStruct((nlb, groups, WIDE, 2 * rows), BF16),
            jax.ShapeDtypeStruct((width, width), BF16),
            jax.ShapeDtypeStruct((width, width), BF16),
        ],
        [
            pltpu.VMEM((nlb * rows, width), BF16),
            pltpu.VMEM((2 * nlb * rows, width), BF16),
            pltpu.VMEM((width, width), BF16),
            pltpu.VMEM((width, width), BF16),
            pltpu.SemaphoreType.DMA((3,)),
        ],
        unread=1,
    )
    g1 = permute(after(f[1], qc), onward)
    m, l, acc = call(
        near_kernel,
        (neighbours,),
        (after(qc, f[1], bands), keys, vals),
        carried_shapes,
        [],
        cost=NEAR_COST,
        room=12,
    )
    g2 = permute(after(f[2], m), onward)
    m, l, acc = call(
        across_kernel,
        (neighbours, half_width),
        (*f, bands, wk, wvt, qc, m, l, acc),
        carried_shapes,
        [pltpu.VMEM(((nlb + 2) * rows, width), BF16), key_scratch, val_scratch, *wide_scratch],
        cost=ACROSS_COST,
    )
    early = nlb // CHUNKS * (CHUNKS - 1)
    early_keys, early_vals = call(
        early_kernel,
        (),
        (after(g0, m), g1, wk, wvt),
        [
            jax.ShapeDtypeStruct((early, groups, rows, WIDE), BF16),
            jax.ShapeDtypeStruct((2, early, groups, WIDE, 2 * rows), BF16),
        ],
        [pltpu.VMEM((early * rows, width), BF16)],
        cost=EARLY_COST,
        room=16,
    )
    e = call(
        payload_kernel,
        (half_width,),
        (*f, g0, g1, g2, after(bands, early_keys)),
        jax.ShapeDtypeStruct(((nlb + 2) * rows, width), BF16),
        [],
        room=6,
    )
    e = permute(e, sibling)
    m, l, acc = call(
        onward_kernel,
        (neighbours, half_width),
        (g2, wk, wvt, qc, early_keys, early_vals, m, l, acc),
        carried_shapes,
        [
            key_scratch,
            val_scratch,
        ],
    )
    return call(
        last_kernel,
        (neighbours, half_width),
        (e, wk, wvt, out_weight, qc, m, l, acc),
        jax.ShapeDtypeStruct(tokens.shape, BF16),
        [
            key_scratch,
            val_scratch,
            *wide_scratch,
            pltpu.VMEM((nlb * rows, width), BF16),
        ],
    )


def solution(mesh):
    return jax.shard_map(
        per_device,
        mesh=mesh,
        in_specs=(P(("groups", "lon"), None, None), P(), P(), P(), P()),
        out_specs=P(("groups", "lon"), None, None),
        check_vma=False,
    )
```
